256 devices in a mesh: row: 32 (over z, y), col: 4 (over x), depth: 2 (over core).
Axes of the slice: x: 4, y: 4, z: 8, core: 2. Of those that a mesh axis runs over, the one named last changes fastest.
Arguments:
- regions: float32 [16384, 1024], P('row'), may hold values from -4 to 4
- captions: float32 [16384, 1024], P(('row', 'col')), may hold values from -4 to 4
- positive: int32 [16384], P('row'), may hold values from 0 to 16383, each once
Outputs:
- mean_objective: float32 [], replicated
- region_grad: float32 [16384, 1024], P(('row', 'col', 'depth'))
- text_derivative: float32 [16384, 1024], P(('row', 'col'))
The draws below stay inside these ranges and needn't reach their ends.
Inputs may be any that keep to these rules, and one draw needn't show every extreme that they name: positive is a permutation: every caption is the match of exactly one region.
All inputs are finite; a program needn't handle non-finite values.
Results may differ from the reference program's by a relative error of at most 0.0015.
The reference program's roundings to bfloat16 on the way count: a program that leaves them out, or rounds other values in their place, can miss the bound.
Values may be sent and summed in bfloat16 or wider, within the bound.
No kernel may reach another device: no remote copies, remote signals or barrier semaphores. Data moves between devices by JAX's collectives and lax.ppermute only.
A program may use at most 192 MiB of HBM per device.

```python
import jax
import jax.numpy as jnp
from jax import lax

FEATURE_LENGTH = 1024
REG_DEV = 512
MATCHED_TOTAL = 16384


def caption_rows(key, lower, upper, strength):
    key_noise, key_scale = jax.random.split(key, 2)
    normal_draw = jax.random.normal(key_noise, (MATCHED_TOTAL, FEATURE_LENGTH), jnp.float32)
    row_scale = jnp.exp(jax.random.uniform(key_scale, (MATCHED_TOTAL, 1), jnp.float32, jnp.log(lower), jnp.log(upper)))
    drawn_rows = normal_draw * row_scale / jnp.sqrt(float(FEATURE_LENGTH))
    row_index = jnp.arange(MATCHED_TOTAL)[:, None]
    spacing = MATCHED_TOTAL // 8
    anchor = jnp.where(row_index % spacing == 0, strength, 0.0)
    twin_mark = jnp.where(row_index % spacing == 1, strength, 0.0)
    anchor_rows = normal_draw * (4.0 / jnp.sqrt(float(FEATURE_LENGTH)))
    mixed = drawn_rows + anchor * (anchor_rows - drawn_rows)
    twin_rows = 0.99 * jnp.roll(mixed, 1, axis=0) + 0.3 * drawn_rows
    mixed = mixed + twin_mark * (twin_rows - mixed)
    return jnp.clip(mixed, -4.0, 4.0)


def region_rows(key, lower, upper, base, span, shared, strength):
    key = jax.random.fold_in(key, 5)
    key_noise, key_scale = jax.random.split(key, 2)
    normal_draw = jax.random.normal(key_noise, (MATCHED_TOTAL, FEATURE_LENGTH), jnp.float32)
    row_scale = jnp.exp(jax.random.uniform(key_scale, (MATCHED_TOTAL, 1), jnp.float32, jnp.log(lower), jnp.log(upper)))
    row_index = jnp.arange(MATCHED_TOTAL)[:, None]
    position = row_index.astype(jnp.float32) / float(MATCHED_TOTAL)
    ramp = base * jnp.exp(jnp.log(span) * position)
    drawn_rows = normal_draw * row_scale * ramp / jnp.sqrt(float(FEATURE_LENGTH))
    spacing = MATCHED_TOTAL // 8
    aligned = jnp.where(row_index % spacing == 3, strength, 0.0)
    factor = 1.0 + 0.25 * (row_index // spacing).astype(jnp.float32)
    target = jnp.roll(shared, 3 + MATCHED_TOTAL // 2, axis=0) * factor
    mixed = drawn_rows + aligned * (target - drawn_rows)
    return jnp.clip(mixed, -4.0, 4.0)


def draw_captions(key, part):
    return caption_rows(key, 0.4, 4.0, 0.0)


def draw_regions(key, part):
    return region_rows(key, 0.4, 4.0, 0.3, 10.0, jnp.zeros((MATCHED_TOTAL, FEATURE_LENGTH), jnp.float32), 0.0)


def setup_inputs(seed: int = 0) -> dict:
    splits = jax.random.split(jax.random.key(seed), 4)
    return {
        "regions": draw_regions(jax.random.fold_in(splits[3], 71), 0),
        "captions": draw_captions(jax.random.fold_in(splits[3], 71), 0),
        "positive": jax.random.permutation(splits[2], MATCHED_TOTAL).astype(jnp.int32),
    }


logit_scaling = 0.07
far_below = -1.0e30


def score_rows(tile_lowbits, text_lowbits):
    return lax.dot_general(tile_lowbits, text_lowbits, (((1,), (1,)), ((), ())), preferred_element_type=jnp.float32) / logit_scaling


def reference(regions, captions, positive):
    region_bf = regions.astype(jnp.bfloat16)
    text_lowbits = captions.astype(jnp.bfloat16)
    block_count = MATCHED_TOTAL // REG_DEV
    region_blocks = region_bf.reshape(block_count, REG_DEV, FEATURE_LENGTH)
    positive_blocks = positive.reshape(block_count, REG_DEV)
    caption_ids = jnp.arange(MATCHED_TOTAL, dtype=jnp.int32)

    def forward(running, inputs):
        col_max, col_sum, positive_sum = running
        tile_lowbits, positive_block = inputs
        scores = score_rows(tile_lowbits, text_lowbits)
        row_max = jnp.max(scores, axis=1)
        row_lse = row_max + jnp.log(jnp.sum(jnp.exp(scores - row_max[:, None]), axis=1))
        new_max = jnp.maximum(col_max, jnp.max(scores, axis=0))
        col_sum = col_sum * jnp.exp(col_max - new_max) + jnp.sum(jnp.exp(scores - new_max[None, :]), axis=0)
        positive_sum = positive_sum + jnp.sum(jnp.where(positive_block[:, None] == caption_ids[None, :], scores, 0.0))
        return (new_max, col_sum, positive_sum), row_lse

    starting = (jnp.full((MATCHED_TOTAL,), far_below, jnp.float32), jnp.zeros((MATCHED_TOTAL,), jnp.float32), jnp.zeros((), jnp.float32))
    (col_max, col_sum, positive_sum), row_lse = lax.scan(forward, starting, (region_blocks, positive_blocks))
    caption_lse = col_max + jnp.log(col_sum)
    mean_objective = (0.5 * (jnp.sum(row_lse) + jnp.sum(caption_lse)) - positive_sum) / MATCHED_TOTAL

    def backward(derivative_total, inputs):
        tile_lowbits, positive_block, lse_block = inputs
        scores = score_rows(tile_lowbits, text_lowbits)
        weight = 0.5 * (jnp.exp(scores - lse_block[:, None]) + jnp.exp(scores - caption_lse[None, :]))
        weight = weight - jnp.where(positive_block[:, None] == caption_ids[None, :], 1.0, 0.0)
        coefficient_lowbits = weight.astype(jnp.bfloat16)
        derivative_tile = jnp.dot(coefficient_lowbits, text_lowbits, preferred_element_type=jnp.float32) / logit_scaling
        derivative_total = derivative_total + lax.dot_general(coefficient_lowbits, tile_lowbits, (((0,), (0,)), ((), ())), preferred_element_type=jnp.float32)
        return derivative_total, derivative_tile

    derivative_total, derivative_tiles = lax.scan(backward, jnp.zeros((MATCHED_TOTAL, FEATURE_LENGTH), jnp.float32), (region_blocks, positive_blocks, row_lse))
    return mean_objective, derivative_tiles.reshape(MATCHED_TOTAL, FEATURE_LENGTH), derivative_total / logit_scaling
```

```python
import functools

import jax
import jax.numpy as jnp
from jax import lax
from jax.experimental import pallas as pl
from jax.experimental.pallas import tpu as pltpu
from jax.sharding import Mesh
from jax.sharding import PartitionSpec as P

logit_scaling = 0.07
far_below = -1e30
head_room = 3.5
tiny = 1e-30
AXES = ("z", "y", "col", "depth")
NZ, NY, NX = 8, 4, 4
FEATURES = 1024
GROUP = 64
BLOCK = 128
TILE = 1024
BF = jnp.bfloat16
F32 = jnp.float32
WIRE = jnp.float16
VMEM = pltpu.VMEM
SMEM = pltpu.SMEM


def index_of(z, y, x, c):
    return ((z % NZ * NY + y % NY) * NX + x % NX) * 2 + c


def moved(value, target):
    pairs = []
    for z in range(NZ):
        for y in range(NY):
            for x in range(NX):
                for c in range(2):
                    to = target(z, y, x, c)
                    if to is not None:
                        pairs.append((index_of(z, y, x, c), index_of(*to)))
    return lax.ppermute(value, AXES, pairs)


def swapped(value):
    return moved(value, lambda z, y, x, c: (z, y, x, 1 - c))


def from_y(value, by):
    return moved(value, lambda z, y, x, c: (z, y - by, x, c))


def from_x(value, by):
    return moved(value, lambda z, y, x, c: (z, y, x - by, c))


def along_z(value, by):
    return moved(value, lambda z, y, x, c: (z + by if c == 0 else z - by, y, x, c))


def call(kernel, outs, *args, limit=48 << 20):
    specs = [
        pl.BlockSpec(memory_space=SMEM if arg.dtype == jnp.int32 else VMEM) for arg in args
    ]
    return pl.pallas_call(
        kernel,
        in_specs=specs,
        out_specs=[pl.BlockSpec(memory_space=VMEM) for _ in outs],
        out_shape=[jax.ShapeDtypeStruct(shape, dtype) for shape, dtype in outs],
        compiler_params=pltpu.CompilerParams(vmem_limit_bytes=limit),
    )(*args)


def place_rows(ref, offset, rows):
    ref[pl.ds(pl.multiple_of(offset, GROUP), GROUP), :] = rows


def column(row):
    return jnp.transpose(jnp.broadcast_to(row, (BLOCK, BLOCK)))


def line(col):
    return jnp.transpose(jnp.broadcast_to(col, (BLOCK, BLOCK)))[0:1, :]


def slot_z(slot, z, c):
    way = 1 - 2 * c
    if slot == 0:
        return z
    if slot <= 3:
        return (z + way * slot + NZ) % NZ
    if slot <= 6:
        return (z - way * (slot - 3) + NZ) % NZ
    return (z + 4) % NZ


def largest(ref):
    best = jnp.abs(ref[0:16, :])
    for start in range(16, TILE, 16):
        best = jnp.maximum(best, jnp.abs(ref[start : start + 16, :]))
    return jnp.max(best.astype(F32))


def score_kernel(
    place, h0, h1, h3, g0, g1, g3, g2, own, near, far, s_out, r_out, c_out, keep, give
):
    z, y, x, c = place[0], place[1], place[2], place[3]

    def put(rows, yy, xx):
        yy, xx = yy % NY, xx % NX
        place_rows(r_out, jnp.where(c == 0, yy * 256 + xx * 64, xx * 256 + yy * 64), rows)

    for ref, by in ((h0, 0), (h1, 1), (h3, 3)):
        for xx in range(NX):
            put(ref[xx * GROUP : (xx + 1) * GROUP, :], y + by, xx)
    for ref, by in ((g0, 0), (g1, 1), (g3, 3), (g2, 2)):
        put(ref[0:GROUP, :], y + 2, x + by)

    c_out[0:128, :] = own[...]
    c_out[128:512, :] = near[0:384, :]
    c_out[512:896, :] = far[0:384, :]
    place_rows(c_out, 896 + c * GROUP, near[384:448, :])
    place_rows(c_out, 896 + (1 - c) * GROUP, far[384:448, :])

    positive = jnp.zeros((8, TILE), F32)
    for ref, by, start in ((h0, 0, 256), (h1, 1, 256), (h3, 3, 256), (g0, 2, 64)):
        coded = ref[start : start + 16, :].astype(F32)
        number = jnp.broadcast_to(coded[0:1, :] * 128.0 + coded[1:2, :], (8, TILE))
        shift = (y + by) % NY * jnp.where(c == 0, 256, 64)
        positive = positive + pltpu.roll(number, shift, 1)
    positive = positive[0:1, :].astype(jnp.int32)

    regions = r_out[...]
    row_max = jnp.full((1, TILE), far_below, F32)
    row_sum = jnp.zeros((1, TILE), F32)
    matched = jnp.zeros((1, TILE), F32)
    cap_maxes = [None] * 8
    cap_sums = [None] * 8
    for slot in range(8):
        chunk = pl.ds(slot * BLOCK, BLOCK)
        scores = lax.dot_general(
            c_out[chunk, :], regions, (((1,), (1,)), ((), ())), preferred_element_type=F32
        ) * (1.0 / logit_scaling)
        s_out[chunk, :] = scores
        owner = slot_z(slot, z, c)
        first = ((owner * NY + y) * NX + x) * BLOCK
        local = positive - first
        ids = lax.broadcasted_iota(jnp.int32, (BLOCK, TILE), 0)
        matched = matched + jnp.sum(
            jnp.where(ids == local, scores, 0.0), axis=0, keepdims=True
        )
        new_max = jnp.maximum(row_max, jnp.max(scores, axis=0, keepdims=True))
        row_sum = row_sum * jnp.exp(row_max - new_max) + jnp.sum(
            jnp.exp(scores - new_max), axis=0, keepdims=True
        )
        row_max = new_max
        cap_max = jnp.max(scores, axis=1, keepdims=True)
        cap_sum = jnp.sum(jnp.exp(scores - cap_max), axis=1, keepdims=True)
        cap_maxes[slot] = line(cap_max)
        cap_sums[slot] = line(cap_sum)

    keep[...] = jnp.zeros((8, TILE), F32)
    give[...] = jnp.zeros((8, TILE), F32)
    for slot in range(8):
        lanes = pl.ds(pl.multiple_of(slot_z(slot, z, c) * BLOCK, BLOCK), BLOCK)
        give[0:1, lanes] = cap_maxes[slot]
        give[2:3, lanes] = cap_sums[slot]
    cap_row_max = give[0:1, :]
    cap_row_sum = give[2:3, :]
    total = jnp.broadcast_to(jnp.sum(matched), (1, TILE))
    caption_top = jnp.broadcast_to(largest(c_out), (1, TILE))
    region_top = jnp.broadcast_to(largest(r_out), (1, TILE))
    zero = jnp.zeros((1, TILE), F32)
    by_row = (row_max, row_sum, total, caption_top)
    by_cap = (cap_row_max, cap_row_sum, zero, region_top)
    for line_at, rows, caps in zip((0, 2, 4, 5), by_row, by_cap):
        keep[line_at : line_at + 1, :] = jnp.where(c == 0, rows, caps)
        give[line_at : line_at + 1, :] = jnp.where(c == 0, caps, rows)


def pair_kernel(place, keep, came, out):
    first = place[3] == 0
    m0, m1, s0, s1 = keep[0:1, :], came[0:1, :], keep[2:3, :], came[2:3, :]
    top = jnp.maximum(m0, m1)
    merged = s0 * jnp.exp(m0 - top) + s1 * jnp.exp(m1 - top)
    zero = jnp.zeros((1, TILE), F32)
    out[0:1, :] = jnp.where(first, m0, top)
    out[1:2, :] = jnp.where(first, m1, zero)
    out[2:3, :] = jnp.where(first, s0, merged)
    out[3:4, :] = jnp.where(first, s1, zero)
    out[4:5, :] = keep[4:5, :] + came[4:5, :]
    out[5:6, :] = jnp.maximum(keep[5:6, :], came[5:6, :])
    out[6:8, :] = jnp.zeros((2, TILE), F32)


def merged_four(own, a, b, opposite):
    maxes = [part[0:2, :] for part in (own, opposite, a, b)]
    top = jnp.maximum(jnp.maximum(maxes[0], maxes[1]), jnp.maximum(maxes[2], maxes[3]))
    parts = [
        part[2:4, :] * jnp.exp(m - top) for part, m in zip((own, opposite, a, b), maxes)
    ]
    sums = (parts[0] + parts[1]) + (parts[2] + parts[3])
    total = (own[4:5, :] + opposite[4:5, :]) + (a[4:5, :] + b[4:5, :])
    peak = jnp.maximum(
        jnp.maximum(own[5:6, :], opposite[5:6, :]), jnp.maximum(a[5:6, :], b[5:6, :])
    )
    return top, sums, total, peak


def four_kernel(own, a, b, opposite, out):
    top, sums, total, peak = merged_four(own[...], a[...], b[...], opposite[...])
    out[0:2, :] = top
    out[2:4, :] = sums
    out[4:5, :] = total
    out[5:6, :] = peak
    out[6:8, :] = jnp.zeros((2, TILE), F32)


def last_kernel(place, own, a, b, opposite, out):
    first = place[3] == 0
    lines = lax.broadcasted_iota(jnp.int32, (8, TILE), 0)
    empty = jnp.where(lines < 2, far_below, 0.0)
    top, sums, total, peak = merged_four(
        own[...],
        a[...],
        jnp.where(first, b[...], empty),
        jnp.where(first, opposite[...], empty),
    )
    lse = top + jnp.log(jnp.where(jnp.logical_or(first, lines[0:2, :] == 0), sums, 1.0))
    both = 0.5 * jnp.sum(lse[0:1, :]) + jnp.where(first, 0.5 * jnp.sum(lse[1:2, :]), 0.0)
    out[0:1, :] = lse[0:1, :]
    out[1:2, :] = jnp.where(first, lse[1:2, :], lse[0:1, :])
    out[2:4, :] = jnp.zeros((2, TILE), F32)
    out[4:5, :] = jnp.broadcast_to(both, (1, TILE)) - total
    out[5:6, :] = peak
    out[6:8, :] = jnp.zeros((2, TILE), F32)


def caption_kernel(
    place, scores, regions, mine, came, h0, h1, h3, g0, w_out, keep, give, own
):
    z, y, x, c = place[0], place[1], place[2], place[3]
    first_core = c == 0
    row_lse = jnp.where(first_core, mine[0:1, :], came[1:2, :])
    region_top = jnp.where(first_core, came[5:6, :], mine[5:6, :])
    scale = head_room / jnp.maximum(region_top, tiny)
    positive = jnp.zeros((8, TILE), F32)
    for ref, by, start in ((h0, 0, 256), (h1, 1, 256), (h3, 3, 256), (g0, 2, 64)):
        coded = ref[start : start + 16, :].astype(F32)
        number = jnp.broadcast_to(coded[0:1, :] * 128.0 + coded[1:2, :], (8, TILE))
        shift = (y + by) % NY * jnp.where(c == 0, 256, 64)
        positive = positive + pltpu.roll(number, shift, 1)
    positive = positive[0:1, :].astype(jnp.int32)
    region_rows = regions[...]
    for slot in (4, 5, 6, 7, 1, 2, 3, 0):
        chunk = pl.ds(slot * BLOCK, BLOCK)
        owner = slot_z(slot, z, c)
        lanes = pl.ds(pl.multiple_of(owner * BLOCK, BLOCK), BLOCK)
        cap_line = jnp.where(first_core, came[1:2, lanes], mine[0:1, lanes])
        cap_lse = jnp.concatenate([column(cap_line)] * 8, axis=1)
        first = ((owner * NY + y) * NX + x) * BLOCK
        ids = lax.broadcasted_iota(jnp.int32, (BLOCK, TILE), 0)
        s = scores[chunk, :]
        weight = 0.5 * (jnp.exp(s - row_lse) + jnp.exp(s - cap_lse))
        weight = weight - jnp.where(ids == positive - first, 1.0, 0.0)
        low = weight.astype(BF)
        w_out[chunk, :] = low
        part = jnp.dot(low, region_rows, preferred_element_type=F32) * scale
        if slot == 0:
            own[...] = part
        elif slot <= 3:
            keep[(slot - 1) * BLOCK : slot * BLOCK, :] = part
        elif slot <= 6:
            give[(slot - 4) * BLOCK : (slot - 3) * BLOCK, :] = part
        else:
            keep[384:448, :] = jnp.where(first_core, part[0:64, :], part[64:128, :])
            give[384:448, :] = jnp.where(first_core, part[64:128, :], part[0:64, :])


def region_kernel(place, weights, captions, mine, came, o0, o1, o3, o2):
    y, x, c = place[1], place[2], place[3]
    first_core = c == 0
    caption_top = jnp.where(first_core, mine[5:6, :], came[5:6, :])
    scale = head_room / jnp.maximum(caption_top, tiny)
    major = jnp.where(first_core, y, x)
    caption_rows = captions[...]
    for ref, by in ((o2, 2), (o1, 1), (o3, 3), (o0, 0)):
        lanes = pl.ds(pl.multiple_of((major + by) % 4 * 256, 256), 256)
        part = lax.dot_general(
            weights[:, lanes], caption_rows, (((0,), (0,)), ((), ())), preferred_element_type=F32
        )
        ref[...] = part * scale


def shards(regions, captions, positive):
    z = lax.axis_index("z")
    y = lax.axis_index("y")
    x = lax.axis_index("col")
    c = lax.axis_index("depth")
    place = jnp.stack([z, y, x, c]).astype(jnp.int32)
    first_core = c == 0
    big = (TILE, FEATURES)

    half = lax.dynamic_index_in_dim(
        regions.reshape(NX, 2, GROUP, FEATURES), c, 1, keepdims=False
    )
    matches = lax.dynamic_index_in_dim(positive.reshape(NX, 2, GROUP), c, 1, keepdims=False)
    packed = jnp.pad(matches.reshape(256), (0, 768))
    spread = jnp.pad(matches, ((0, 0), (0, 192))).reshape(TILE)
    row = jnp.where(first_core, packed, spread)
    coded = jnp.pad(jnp.stack([row // 128, row % 128]), ((0, 14), (0, 0))).astype(BF)
    own_half = jnp.concatenate([half.reshape(256, FEATURES).astype(BF), coded], axis=0)
    own_group = jnp.concatenate(
        [
            lax.dynamic_index_in_dim(half, x, 0, keepdims=False).astype(BF),
            coded,
        ],
        axis=0,
    )
    text = captions.astype(BF)

    two = along_z(text, -2)
    g0 = from_y(own_group, 2)
    one = along_z(text, -1)
    h1 = from_y(own_half, 1)
    h3 = from_y(own_half, 3)
    three = along_z(two, -1)
    four = along_z(lax.dynamic_slice_in_dim(two, c * GROUP, GROUP, 0), -2)
    group = g0[0:GROUP]
    g1 = from_x(group, 1)
    g3 = from_x(group, 3)
    g2 = from_x(group, 2)
    near = jnp.concatenate([one, two, three, four], axis=0)
    far = swapped(near)

    scores, region_rows, caption_rows, keep, give = call(
        score_kernel,
        [(big, F32), (big, BF), (big, BF), ((8, TILE), F32), ((8, TILE), F32)],
        place, own_half, h1, h3, g0, g1, g3, g2, text, near, far,
    )

    small = [((8, TILE), F32)]
    (stats,) = call(pair_kernel, small, place, keep, swapped(give))

    def stage_one(by_y, by_z):
        return moved(
            stats, lambda z, y, x, c: (z, y - by_y, x, c) if c == 0 else (z - by_z, y, x, c)
        )

    (stats,) = call(
        four_kernel, small, stats, stage_one(1, 2), stage_one(3, 6), stage_one(2, 4)
    )
    a = moved(stats, lambda z, y, x, c: (z, y, x - 1, c) if c == 0 else (z ^ 1, y, x, c))
    b = moved(stats, lambda z, y, x, c: (z, y, x - 3, c) if c == 0 else None)
    opposite = moved(stats, lambda z, y, x, c: (z, y, x - 2, c) if c == 0 else None)
    (lse,) = call(last_kernel, small, place, stats, a, b, opposite)
    came = swapped(lse)

    weights, keep, give, own = call(
        caption_kernel,
        [(big, BF), ((448, FEATURES), F32), ((448, FEATURES), F32), ((BLOCK, FEATURES), F32)],
        place, scores, region_rows, lse, came, own_half, h1, h3, g0,
    )
    got = swapped(give.astype(WIRE))
    quarter = ((256, FEATURES), F32)
    r0, r1, r3, r2 = call(
        region_kernel, [quarter] * 4, place, weights, caption_rows, lse, came
    )

    def major_from(value, by):
        return moved(
            value, lambda z, y, x, c: (z, y + by, x, c) if c == 0 else (z, y, x + by, c)
        )

    def minor_from(value, by):
        return moved(
            value, lambda z, y, x, c: (z, y, x + by, c) if c == 0 else (z, y + by, x, c)
        )

    q2 = major_from(r2.astype(WIRE), 2)
    q1 = major_from(r1.astype(WIRE), 1)
    q3 = major_from(r3.astype(WIRE), 3)

    total = keep + got.astype(F32)
    ahead = along_z(
        jnp.concatenate([total[0:128], total[256:384]], axis=0).astype(WIRE), 1
    )
    skipped = along_z(total[384:448].astype(WIRE), 2)
    summed = ((r0 + q2.astype(F32)) + (q1.astype(F32) + q3.astype(F32))).reshape(
        4, GROUP, FEATURES
    )
    minor = jnp.where(first_core, x, y)

    def piece(by):
        return lax.dynamic_index_in_dim(summed, (minor + by) % 4, 0, keepdims=False)

    t2 = minor_from(piece(2).astype(WIRE), 2)
    t1 = minor_from(piece(1).astype(WIRE), 1)
    t3 = minor_from(piece(3).astype(WIRE), 3)
    skipped_rows = lax.dynamic_update_slice_in_dim(
        jnp.zeros((BLOCK, FEATURES), F32), skipped.astype(F32), c * GROUP, 0
    )
    onward = total[128:256] + ahead[128:256].astype(F32) + skipped_rows
    passed = along_z(onward.astype(WIRE), 2)
    mine = own + ahead[0:128].astype(F32) + passed.astype(F32)

    share = lse[4:5, 0:128] * jnp.ones((8, 1), F32)
    for bit in range(4):
        def partner(z, y, x, c, bit=bit):
            if c == 0:
                return (z ^ (1 << bit), y, x, c) if bit < 3 else None
            return (z, y ^ (1 << bit), x, c) if bit < 2 else (z, y, x ^ (1 << (bit - 2)), c)

        share = share + moved(share, partner)
    share = share + swapped(share)
    mean_objective = share[0, 0] / (NZ * NY * regions.shape[0])

    caption_top = jnp.where(first_core, lse[5, 0], came[5, 0])
    region_top = jnp.where(first_core, came[5, 0], lse[5, 0])
    unscale = 1.0 / (head_room * logit_scaling)
    region_grad = ((piece(0) + t2.astype(F32)) + (t1.astype(F32) + t3.astype(F32))) * (
        jnp.maximum(caption_top, tiny) * unscale
    )
    text_derivative = (mine + swapped(mine)) * (jnp.maximum(region_top, tiny) * unscale)
    return mean_objective, region_grad, text_derivative


def solution(mesh):
    grid = Mesh(mesh.devices.reshape(NZ, NY, NX, 2), AXES)
    return jax.shard_map(
        shards,
        mesh=grid,
        in_specs=(P(("z", "y"), None), P(("z", "y", "col"), None), P(("z", "y"))),
        out_specs=(
            P(),
            P(("z", "y", "col", "depth"), None),
            P(("z", "y", "col"), None),
        ),
        check_vma=False,
    )
```

```python
import functools

import jax
import jax.numpy as jnp
from jax import lax
from jax.experimental import pallas as pl
from jax.experimental.pallas import tpu as pltpu
from jax.sharding import Mesh
from jax.sharding import PartitionSpec as P

logit_scaling = 0.07
far_below = -1e30
head_room = 3.5
tiny = 1e-30
AXES = ("z", "y", "col", "depth")
NZ, NY, NX = 8, 4, 4
FEATURES = 1024
GROUP = 64
BLOCK = 128
TILE = 1024
BF = jnp.bfloat16
F32 = jnp.float32
WIRE = jnp.float16
VMEM = pltpu.VMEM
SMEM = pltpu.SMEM


def index_of(z, y, x, c):
    return ((z % NZ * NY + y % NY) * NX + x % NX) * 2 + c


def moved(value, target):
    pairs = []
    for z in range(NZ):
        for y in range(NY):
            for x in range(NX):
                for c in range(2):
                    to = target(z, y, x, c)
                    if to is not None:
                        pairs.append((index_of(z, y, x, c), index_of(*to)))
    return lax.ppermute(value, AXES, pairs)


def swapped(value):
    return moved(value, lambda z, y, x, c: (z, y, x, 1 - c))


def from_y(value, by):
    return moved(value, lambda z, y, x, c: (z, y - by, x, c))


def from_x(value, by):
    return moved(value, lambda z, y, x, c: (z, y, x - by, c))


def along_z(value, by):
    return moved(value, lambda z, y, x, c: (z + by if c == 0 else z - by, y, x, c))


def call(kernel, outs, *args, limit=12 << 20, scratch=(), us=1.0):
    specs = [pl.BlockSpec(memory_space=SMEM if arg.ndim == 1 else VMEM) for arg in args]
    return pl.pallas_call(
        kernel,
        in_specs=specs,
        out_specs=[pl.BlockSpec(memory_space=VMEM) for _ in outs],
        out_shape=[jax.ShapeDtypeStruct(shape, dtype) for shape, dtype in outs],
        scratch_shapes=scratch,
        cost_estimate=pl.CostEstimate(
            flops=int(us * 1.1e9), bytes_accessed=int(us * 3e6), transcendentals=0
        ),
        compiler_params=pltpu.CompilerParams(vmem_limit_bytes=limit),
    )(*args)


def place_rows(ref, offset, rows):
    ref[pl.ds(pl.multiple_of(offset, GROUP), GROUP), :] = rows


def column(row):
    return jnp.transpose(jnp.broadcast_to(row, (BLOCK, BLOCK)))


def line(col):
    return jnp.transpose(jnp.broadcast_to(col, (BLOCK, BLOCK)))[0:1, :]


WAYS = (-1, -3, -2, 4, 1, 3, 2, 0)


def slot_z(slot, z, c):
    return (z + (1 - 2 * c) * WAYS[slot] + NZ) % NZ


def positives(place, own, full, far, pair):
    y, x, c = place[1], place[2], place[3]
    positive = jnp.zeros((8, TILE), F32)
    for ref, by, start in (
        (own, 0, 512),
        (full, 1 + 2 * c, 512),
        (far, 3 - 2 * c, 258),
        (pair, 2, 128),
    ):
        base = start // 16 * 16
        coded = ref[base : base + 16, :].astype(F32)
        at = start - base
        number = jnp.broadcast_to(
            coded[at : at + 1, :] * 128.0 + coded[at + 1 : at + 2, :], (8, TILE)
        )
        shift = jnp.where(c == 0, by * 256, (y + by) % NY * 64 + TILE - x * 256)
        positive = positive + pltpu.roll(number, shift % TILE, 1)
    return positive[0:1, :].astype(jnp.int32)


def largest(ref):
    best = jnp.abs(ref[0:16, :])
    for start in range(16, TILE, 16):
        best = jnp.maximum(best, jnp.abs(ref[start : start + 16, :]))
    return jnp.max(best.astype(F32))


def coded_matches(place, matches):
    c = place[3]
    lane = lax.broadcasted_iota(jnp.int32, (8, TILE), 1)
    at = lax.broadcasted_iota(jnp.int32, (8, TILE), 0)
    coded = jnp.zeros((8, TILE), F32)
    for step in range(2):
        which = c if step == 0 else 1 - c
        wide = jnp.zeros((8, TILE), F32)
        for xx in range(NX):
            line_of = jnp.concatenate(
                [
                    jnp.broadcast_to(matches[xx : xx + 1, :].astype(F32), (8, BLOCK)),
                    jnp.zeros((8, TILE - BLOCK), F32),
                ],
                axis=1,
            )
            mine = jnp.logical_and(lane >= which * GROUP, lane < which * GROUP + GROUP)
            shift = TILE - which * GROUP + xx * jnp.where(which == 0, 64, 256)
            wide = wide + pltpu.roll(jnp.where(mine, line_of, 0.0), shift % TILE, 1)
        high = jnp.floor(wide * (1.0 / 128.0))
        low = wide - high * 128.0
        coded = jnp.where(at == 2 * step, high, jnp.where(at == 2 * step + 1, low, coded))
    return jnp.concatenate([coded, jnp.zeros((8, TILE), F32)], axis=0).astype(BF)


def part_kernel(place, regions, matches, part):
    x, c = place[2], place[3]
    for at in range(2):
        start = pl.multiple_of(((x % 2 * 2 + at) * 2 + c) * GROUP, GROUP)
        part[at * GROUP : (at + 1) * GROUP, :] = regions[pl.ds(start, GROUP), :].astype(BF)
    part[128:144, :] = coded_matches(place, matches)


def whole_kernel(place, regions, part, whole):
    c = place[3]
    whole[512:528, :] = part[128:144, :]
    for step in range(2):
        which = c if step == 0 else 1 - c
        for xx in range(NX):
            start = pl.multiple_of((xx * 2 + which) * GROUP, GROUP)
            to = (step * NX + xx) * GROUP
            whole[to : to + GROUP, :] = regions[pl.ds(start, GROUP), :].astype(BF)


def text_kernel(captions, text):
    text[...] = captions[...].astype(BF)


def skip_kernel(place, one, two, out):
    out[0:128, :] = one[...]
    out[128:192, :] = two[pl.ds(pl.multiple_of(place[3] * GROUP, GROUP), GROUP), :]


def score_kernel(
    place, own, full, far, pair, other, text, one, two, skip, s_out, r_out, c_out, keep, give
):
    z, y, x, c = place[0], place[1], place[2], place[3]

    def put(by, xx, rows):
        offset = jnp.where(
            c == 0, by * 256 + xx * 64, (xx + NX - x) % NX * 256 + (y + by) % NY * 64
        )
        place_rows(r_out, offset, rows)

    for ref, by in ((own, 0), (full, 1 + 2 * c), (far, 3 - 2 * c)):
        for xx in range(NX):
            put(by, xx, ref[xx * GROUP : (xx + 1) * GROUP, :])
    for at in range(2):
        rows = pl.ds(at * GROUP, GROUP)
        put(2, x % 2 * 2 + at, pair[rows, :])
        put(2, (1 - x % 2) * 2 + at, other[rows, :])
    c_out[0:128, :] = far[272:400, :]
    c_out[128:256, :] = far[528:656, :]
    c_out[256:384, :] = far[400:528, :]
    place_rows(c_out, 384 + c * GROUP, skip[128:192, :])
    place_rows(c_out, 384 + (1 - c) * GROUP, far[656:720, :])
    c_out[512:640, :] = one[...]
    c_out[640:768, :] = skip[0:128, :]
    c_out[768:896, :] = two[...]
    c_out[896:1024, :] = text[...]

    positive = positives(place, own, full, far, pair)
    regions = r_out[...]
    for part in range(2):
        chunk = pl.ds(part * 512, 512)
        s_out[chunk, :] = lax.dot_general(
            c_out[chunk, :], regions, (((1,), (1,)), ((), ())), preferred_element_type=F32
        ) * (1.0 / logit_scaling)

    row_max = jnp.full((1, TILE), far_below, F32)
    row_sum = jnp.zeros((1, TILE), F32)
    matched = jnp.zeros((1, TILE), F32)
    ids = lax.broadcasted_iota(jnp.int32, (BLOCK, TILE), 0)
    for slot in range(8):
        scores = s_out[slot * BLOCK : (slot + 1) * BLOCK, :]
        owner = slot_z(slot, z, c)
        first = ((owner * NY + y) * NX + x) * BLOCK
        matched = matched + jnp.sum(
            jnp.where(ids == positive - first, scores, 0.0), axis=0, keepdims=True
        )
        new_max = jnp.maximum(row_max, jnp.max(scores, axis=0, keepdims=True))
        row_sum = row_sum * jnp.exp(row_max - new_max) + jnp.sum(
            jnp.exp(scores - new_max), axis=0, keepdims=True
        )
        row_max = new_max
        cap_max = jnp.max(scores, axis=1, keepdims=True)
        cap_sum = jnp.sum(jnp.exp(scores - cap_max), axis=1, keepdims=True)
        lanes = pl.ds(pl.multiple_of(owner * BLOCK, BLOCK), BLOCK)
        give[0:1, lanes] = line(cap_max)
        give[2:3, lanes] = line(cap_sum)

    cap_row_max = give[0:1, :]
    cap_row_sum = give[2:3, :]
    total = jnp.broadcast_to(jnp.sum(matched), (1, TILE))
    caption_top = jnp.broadcast_to(largest(c_out), (1, TILE))
    region_top = jnp.broadcast_to(largest(r_out), (1, TILE))
    zero = jnp.zeros((1, TILE), F32)
    two_zeros = jnp.zeros((2, TILE), F32)
    turned = jnp.concatenate([row_max, zero, row_sum, zero, total, caption_top, two_zeros], axis=0)
    turned = pltpu.roll(turned, jnp.where(c == 0, y, x) * 256, 1)
    by_cap = jnp.concatenate(
        [cap_row_max, zero, cap_row_sum, zero, zero, region_top, two_zeros], axis=0
    )
    keep[...] = jnp.where(c == 0, turned, by_cap)
    give[...] = jnp.where(c == 0, by_cap, turned)


def pair_kernel(place, keep, came, out):
    first = place[3] == 0
    m0, m1, s0, s1 = keep[0:1, :], came[0:1, :], keep[2:3, :], came[2:3, :]
    top = jnp.maximum(m0, m1)
    merged = s0 * jnp.exp(m0 - top) + s1 * jnp.exp(m1 - top)
    zero = jnp.zeros((1, TILE), F32)
    out[0:1, :] = jnp.where(first, m0, top)
    out[1:2, :] = jnp.where(first, m1, zero)
    out[2:3, :] = jnp.where(first, s0, merged)
    out[3:4, :] = jnp.where(first, s1, zero)
    out[4:5, :] = keep[4:5, :] + came[4:5, :]
    out[5:6, :] = jnp.maximum(keep[5:6, :], came[5:6, :])
    out[6:8, :] = jnp.zeros((2, TILE), F32)


def merged(own, came):
    top = jnp.maximum(own[0:2, :], came[0:2, :])
    sums = own[2:4, :] * jnp.exp(own[0:2, :] - top) + came[2:4, :] * jnp.exp(came[0:2, :] - top)
    return top, sums, own[4:5, :] + came[4:5, :], jnp.maximum(own[5:6, :], came[5:6, :])


def merge_kernel(own, came, out):
    top, sums, total, peak = merged(own[...], came[...])
    out[0:2, :] = top
    out[2:4, :] = sums
    out[4:5, :] = total
    out[5:6, :] = peak
    out[6:8, :] = jnp.zeros((2, TILE), F32)


def last_kernel(place, own, came, out):
    first = place[3] == 0
    lines = lax.broadcasted_iota(jnp.int32, (8, TILE), 0)
    empty = jnp.where(lines < 2, far_below, 0.0)
    top, sums, total, peak = merged(own[...], jnp.where(first, came[...], empty))
    lse = top + jnp.log(jnp.where(jnp.logical_or(first, lines[0:2, :] == 0), sums, 1.0))
    both = 0.5 * jnp.sum(lse[0:1, :]) + jnp.where(first, 0.5 * jnp.sum(lse[1:2, :]), 0.0)
    out[0:1, :] = lse[0:1, :]
    out[1:2, :] = jnp.where(first, lse[1:2, :], lse[0:1, :])
    out[2:4, :] = jnp.zeros((2, TILE), F32)
    out[4:5, :] = jnp.broadcast_to(both, (1, TILE)) - total
    out[5:6, :] = peak
    out[6:8, :] = jnp.zeros((2, TILE), F32)


def weight_kernel(
    place, scores, regions, mine, came, whole, full, far, pair, w_out, give, kept
):
    z, y, x, c = place[0], place[1], place[2], place[3]
    first_core = c == 0
    row_lse = jnp.where(first_core, mine[0:1, :], came[1:2, :])
    turn = (NX - jnp.where(first_core, y, x)) % NX * 256
    row_lse = pltpu.roll(jnp.broadcast_to(row_lse, (8, TILE)), turn, 1)[0:1, :]
    positive = positives(place, whole, full, far, pair)
    ids = lax.broadcasted_iota(jnp.int32, (BLOCK, TILE), 0)
    for slot in range(8):
        chunk = pl.ds(slot * BLOCK, BLOCK)
        owner = slot_z(slot, z, c)
        lanes = pl.ds(pl.multiple_of(owner * BLOCK, BLOCK), BLOCK)
        cap_line = jnp.where(first_core, came[1:2, lanes], mine[0:1, lanes])
        cap_lse = jnp.concatenate([column(cap_line)] * 8, axis=1)
        first = ((owner * NY + y) * NX + x) * BLOCK
        s = scores[chunk, :]
        weight = 0.5 * (jnp.exp(s - row_lse) + jnp.exp(s - cap_lse))
        weight = weight - jnp.where(ids == positive - first, 1.0, 0.0)
        w_out[chunk, :] = weight.astype(BF)
    scale = region_scale(place, mine, came)
    part = jnp.dot(w_out[0:512, :], regions[...], preferred_element_type=F32) * scale
    nothing = jnp.zeros((16, TILE), F32)
    for at in range(3):
        start = at * 144
        give[start : start + 128, :] = part[at * 128 : (at + 1) * 128, :]
        give[start + 128 : start + 144, :] = nothing
    give[432:496, :] = jnp.where(first_core, part[448:512, :], part[384:448, :])
    give[496:512, :] = nothing
    kept[0:64, :] = jnp.where(first_core, part[384:448, :], part[448:512, :])
    kept[64:80, :] = digits(jnp.where(first_core, mine[4:5, :], came[4:5, :]), z)


def digits(value, index):
    high = jnp.floor(value * 2.0**-20)
    rest = value - high * 2.0**20
    middle = jnp.floor(rest * 2.0**-10)
    rest = rest - middle * 2.0**10
    low = jnp.floor(rest)
    last = jnp.floor((rest - low) * 2.0**10)
    lane = lax.broadcasted_iota(jnp.int32, (16, TILE), 1)
    line_at = lax.broadcasted_iota(jnp.int32, (16, TILE), 0)
    which = lane // 16
    digit = jnp.where(
        which == 0, high, jnp.where(which == 1, middle, jnp.where(which == 2, low, last))
    )
    here = jnp.logical_and(line_at == 0, jnp.logical_and(lane < 64, lane % 16 == index))
    return jnp.where(here, digit, 0.0)


def region_scale(place, mine, came):
    region_top = jnp.where(place[3] == 0, came[5:6, :], mine[5:6, :])
    return head_room / jnp.maximum(region_top, tiny)


def caption_kernel(place, weights, regions, mine, came, near_two, second, own):
    first_core = place[3] == 0
    part = jnp.dot(
        weights[512:1024, :], regions[...], preferred_element_type=F32
    ) * region_scale(place, mine, came)
    code = digits(jnp.where(first_core, mine[4:5, :], came[4:5, :]), place[0])
    near_two[0:128, :] = part[0:128, :]
    near_two[128:144, :] = code
    near_two[144:272, :] = part[128:256, :]
    near_two[272:288, :] = code
    second[0:128, :] = part[256:384, :]
    second[128:144, :] = code
    own[0:128, :] = part[384:512, :]
    own[128:144, :] = jnp.where(first_core, code, 0.0)


def region_kernel(place, weights, captions, mine, came, o0, o1, o2, o3):
    first_core = place[3] == 0
    caption_top = jnp.where(first_core, mine[5:6, :], came[5:6, :])
    scale = head_room / jnp.maximum(caption_top, tiny)
    code = digits(
        jnp.where(first_core, came[4:5, :], mine[4:5, :]), place[1] * NX + place[2]
    )
    part = lax.dot_general(
        weights[...], captions[...], (((0,), (0,)), ((), ())), preferred_element_type=F32
    )
    for by, ref in enumerate((o0, o1, o2, o3)):
        ref[0:256, :] = part[by * 256 : (by + 1) * 256, :] * scale
        ref[256:272, :] = code


def shards(regions, captions, positive):
    z = lax.axis_index("z")
    y = lax.axis_index("y")
    x = lax.axis_index("col")
    c = lax.axis_index("depth")
    place = jnp.stack([z, y, x, c]).astype(jnp.int32)
    first_core = c == 0
    big = (TILE, FEATURES)

    (part,) = call(
        part_kernel, [((144, FEATURES), BF)], place, regions, positive.reshape(NX, BLOCK)
    )
    (whole,) = call(whole_kernel, [((528, FEATURES), BF)], place, regions, part, us=40.0)
    (text,) = call(text_kernel, [((BLOCK, FEATURES), BF)], captions)

    full = moved(whole, lambda z, y, x, c: (z, y - 1 if c == 0 else y + 1, x, c))
    pair = from_y(part, 2)
    other = moved(pair[0:128], lambda z, y, x, c: (z, y, x ^ 1, c))
    one = along_z(text, -1)
    two = along_z(text, -2)
    (passed,) = call(skip_kernel, [((192, FEATURES), BF)], place, one, two, us=40.0)
    skip = along_z(passed, -2)
    full, other, skip = lax.optimization_barrier((full, other, skip))
    far = swapped(jnp.concatenate([full[256:528], one, two, skip], axis=0))

    scores, region_rows, caption_rows, keep, give = call(
        score_kernel,
        [(big, F32), (big, BF), (big, BF), ((8, TILE), F32), ((8, TILE), F32)],
        place, whole, full, far, pair, other, text, one, two, skip,
        us=8.0,
    )

    small = [((8, TILE), F32)]
    (stats,) = call(pair_kernel, small, place, keep, swapped(give))

    def partner(bit):
        def target(z, y, x, c):
            if c == 1:
                return (z ^ (1 << bit), y, x, c) if bit < 3 else None
            return (z, y ^ (1 << bit), x, c) if bit < 2 else (z, y, x ^ (1 << (bit - 2)), c)

        return target

    for bit in range(3):
        (stats,) = call(merge_kernel, small, stats, moved(stats, partner(bit)))
    (lse,) = call(last_kernel, small, place, stats, moved(stats, partner(3)))
    came = swapped(lse)

    weights, give, kept_half = call(
        weight_kernel,
        [(big, BF), ((512, FEATURES), F32), ((80, FEATURES), F32)],
        place, scores, region_rows, lse, came, whole, full, far, pair,
        us=40.0,
    )
    got = swapped(give.astype(WIRE))
    near_two, second, own = call(
        caption_kernel,
        [((288, FEATURES), F32), ((144, FEATURES), F32), ((144, FEATURES), F32)],
        place, weights, region_rows, lse, came,
        us=20.0,
    )
    near_two = (near_two + got[0:288].astype(F32)).astype(WIRE)
    kept_half = (kept_half + got[432:512].astype(F32)).astype(WIRE)
    weights, near_two, kept_half = lax.optimization_barrier((weights, near_two, kept_half))
    ahead = along_z(near_two, 1)
    opposite = along_z(kept_half, 4)
    r0, r1, r2, r3 = call(
        region_kernel, [((272, FEATURES), F32)] * 4, place, weights, caption_rows, lse, came, us=30.0
    )
    r1, r2, r3, ahead = lax.optimization_barrier(
        (r1.astype(WIRE), r2.astype(WIRE), r3.astype(WIRE), ahead)
    )

    def major_from(value, by):
        return moved(
            value, lambda z, y, x, c: (z, y + by, x, c) if c == 0 else (z, y, x + by, c)
        )

    def minor_from(value, by):
        return moved(
            value, lambda z, y, x, c: (z, y, x + by, c) if c == 0 else (z, y + by, x, c)
        )

    onward = (second + got[288:432].astype(F32)) + ahead[144:288].astype(F32)
    passed = along_z(onward.astype(WIRE), 2)
    q2 = major_from(r2, 2)
    q1 = major_from(r1, 1)
    q3 = major_from(r3, 3)
    summed = (r0 + q2.astype(F32)) + (q1.astype(F32) + q3.astype(F32))
    summed, passed, opposite = lax.optimization_barrier((summed, passed, opposite))
    blocks = summed[0:256].reshape(4, GROUP, FEATURES)
    minor = jnp.where(first_core, x, y)

    def piece(by):
        block = lax.dynamic_index_in_dim(blocks, (minor + by) % 4, 0, keepdims=False)
        return jnp.concatenate([block, summed[256:272]], axis=0)

    t2, t1, t3 = (minor_from(piece(by).astype(WIRE), by) for by in (2, 1, 3))
    nothing = jnp.zeros((GROUP, FEATURES), F32)
    late = opposite.astype(F32)
    late = jnp.where(
        first_core,
        jnp.concatenate([late[0:64], nothing, late[64:80]], axis=0),
        jnp.concatenate([nothing, late[0:64], nothing[0:16]], axis=0),
    )
    mine = (own + ahead[0:144].astype(F32)) + (passed.astype(F32) + late)
    both = mine + swapped(mine)
    all_regions = (piece(0) + t2.astype(F32)) + (t1.astype(F32) + t3.astype(F32))

    caption_top = jnp.where(first_core, lse[5:6, :], came[5:6, :])
    region_top = jnp.where(first_core, came[5:6, :], lse[5:6, :])
    unscale = 1.0 / (head_room * logit_scaling)
    region_grad = all_regions[0:64] * (jnp.maximum(caption_top, tiny) * unscale)
    text_derivative = both[0:128] * (jnp.maximum(region_top, tiny) * unscale)
    numbers = both[128:136, 0:128] + all_regions[64:72, 0:128]
    worth = jnp.exp2(20.0 - 10.0 * (jnp.arange(128) // 16).astype(F32))
    worth = jnp.where(jnp.arange(128) < 64, worth, 0.0)
    mean_objective = jnp.sum(numbers * worth[None, :]) / (NZ * NY * regions.shape[0])
    return mean_objective, region_grad, text_derivative


def solution(mesh):
    grid = Mesh(mesh.devices.reshape(NZ, NY, NX, 2), AXES)
    return jax.shard_map(
        shards,
        mesh=grid,
        in_specs=(P(("z", "y"), None), P(("z", "y", "col"), None), P(("z", "y"))),
        out_specs=(
            P(),
            P(("z", "y", "col", "depth"), None),
            P(("z", "y", "col"), None),
        ),
        check_vma=False,
    )
```

```python
import functools

import jax
import jax.numpy as jnp
from jax import lax
from jax.experimental import pallas as pl
from jax.experimental.pallas import tpu as pltpu
from jax.sharding import Mesh
from jax.sharding import PartitionSpec as P

logit_scaling = 0.07
far_below = -1e30
head_room = 3.5
tiny = 1e-30
AXES = ("z", "y", "col", "depth")
NZ, NY, NX = 8, 4, 4
FEATURES = 1024
GROUP = 64
BLOCK = 128
TILE = 1024
BF = jnp.bfloat16
F32 = jnp.float32
WIRE = jnp.float16
VMEM = pltpu.VMEM
SMEM = pltpu.SMEM


def index_of(z, y, x, c):
    return ((z % NZ * NY + y % NY) * NX + x % NX) * 2 + c


def moved(value, target):
    pairs = []
    for z in range(NZ):
        for y in range(NY):
            for x in range(NX):
                for c in range(2):
                    to = target(z, y, x, c)
                    if to is not None:
                        pairs.append((index_of(z, y, x, c), index_of(*to)))
    return lax.ppermute(value, AXES, pairs)


def swapped(value):
    return moved(value, lambda z, y, x, c: (z, y, x, 1 - c))


def from_y(value, by):
    return moved(value, lambda z, y, x, c: (z, y - by, x, c))


def from_x(value, by):
    return moved(value, lambda z, y, x, c: (z, y, x - by, c))


def along_z(value, by):
    return moved(value, lambda z, y, x, c: (z + by if c == 0 else z - by, y, x, c))


def call(kernel, outs, *args, limit=1 << 20, us=1.0):
    specs = [pl.BlockSpec(memory_space=SMEM if arg.ndim == 1 else VMEM) for arg in args]
    return pl.pallas_call(
        kernel,
        in_specs=specs,
        out_specs=[pl.BlockSpec(memory_space=VMEM) for _ in outs],
        out_shape=[jax.ShapeDtypeStruct(shape, dtype) for shape, dtype in outs],
        cost_estimate=pl.CostEstimate(
            flops=int(us * 1.1e9), bytes_accessed=int(us * 3e6), transcendentals=0
        ),
        compiler_params=pltpu.CompilerParams(vmem_limit_bytes=limit),
    )(*args)


def place_rows(ref, offset, rows):
    ref[pl.ds(pl.multiple_of(offset, GROUP), GROUP), :] = rows


def column(row):
    return jnp.transpose(jnp.broadcast_to(row, (BLOCK, BLOCK)))


def line(col):
    return jnp.transpose(jnp.broadcast_to(col, (BLOCK, BLOCK)))[0:1, :]


WAYS = (-1, -3, -2, 4, 1, 3, 2, 0)


def slot_z(slot, z, c):
    return (z + (1 - 2 * c) * WAYS[slot] + NZ) % NZ


def positives(place, own, full, far, pair):
    y, x, c = place[1], place[2], place[3]
    positive = jnp.zeros((8, TILE), F32)
    for ref, by, start in (
        (own, 0, 512),
        (full, 1 + 2 * c, 512),
        (far, 3 - 2 * c, 258),
        (pair, 2, 128),
    ):
        base = start // 16 * 16
        coded = ref[base : base + 16, :].astype(F32)
        at = start - base
        number = jnp.broadcast_to(
            coded[at : at + 1, :] * 128.0 + coded[at + 1 : at + 2, :], (8, TILE)
        )
        shift = jnp.where(c == 0, by * 256, (y + by) % NY * 64 + TILE - x * 256)
        positive = positive + pltpu.roll(number, shift % TILE, 1)
    return positive[0:1, :].astype(jnp.int32)


def largest(ref):
    best = jnp.abs(ref[0:16, :])
    for start in range(16, TILE, 16):
        best = jnp.maximum(best, jnp.abs(ref[start : start + 16, :]))
    return jnp.max(best.astype(F32))


def coded_matches(place, matches):
    c = place[3]
    lane = lax.broadcasted_iota(jnp.int32, (8, TILE), 1)
    at = lax.broadcasted_iota(jnp.int32, (8, TILE), 0)
    coded = jnp.zeros((8, TILE), F32)
    for step in range(2):
        which = c if step == 0 else 1 - c
        wide = jnp.zeros((8, TILE), F32)
        for xx in range(NX):
            line_of = jnp.concatenate(
                [
                    jnp.broadcast_to(matches[xx : xx + 1, :].astype(F32), (8, BLOCK)),
                    jnp.zeros((8, TILE - BLOCK), F32),
                ],
                axis=1,
            )
            mine = jnp.logical_and(lane >= which * GROUP, lane < which * GROUP + GROUP)
            shift = TILE - which * GROUP + xx * jnp.where(which == 0, 64, 256)
            wide = wide + pltpu.roll(jnp.where(mine, line_of, 0.0), shift % TILE, 1)
        high = jnp.floor(wide * (1.0 / 128.0))
        low = wide - high * 128.0
        coded = jnp.where(at == 2 * step, high, jnp.where(at == 2 * step + 1, low, coded))
    return jnp.concatenate([coded, jnp.zeros((8, TILE), F32)], axis=0).astype(BF)


def part_kernel(place, regions, matches, part):
    x, c = place[2], place[3]
    for at in range(2):
        start = pl.multiple_of(((x % 2 * 2 + at) * 2 + c) * GROUP, GROUP)
        part[at * GROUP : (at + 1) * GROUP, :] = regions[pl.ds(start, GROUP), :].astype(BF)
    part[128:144, :] = coded_matches(place, matches)


def whole_kernel(place, regions, part, whole):
    c = place[3]
    whole[512:528, :] = part[128:144, :]
    for step in range(2):
        which = c if step == 0 else 1 - c
        for xx in range(NX):
            start = pl.multiple_of((xx * 2 + which) * GROUP, GROUP)
            to = (step * NX + xx) * GROUP
            whole[to : to + GROUP, :] = regions[pl.ds(start, GROUP), :].astype(BF)


def text_kernel(captions, text):
    text[...] = captions[...].astype(BF)


def skip_kernel(place, one, two, out):
    out[0:128, :] = one[...]
    out[128:192, :] = two[pl.ds(pl.multiple_of(place[3] * GROUP, GROUP), GROUP), :]


def score_kernel(
    place, own, full, far, pair, other, text, one, two, skip, s_out, r_out, c_out, p_out, keep, give
):
    z, y, x, c = place[0], place[1], place[2], place[3]

    def put(by, xx, rows):
        offset = jnp.where(
            c == 0, by * 256 + xx * 64, (xx + NX - x) % NX * 256 + (y + by) % NY * 64
        )
        place_rows(r_out, offset, rows)

    for ref, by in ((own, 0), (full, 1 + 2 * c), (far, 3 - 2 * c)):
        for xx in range(NX):
            put(by, xx, ref[xx * GROUP : (xx + 1) * GROUP, :])
    for at in range(2):
        rows = pl.ds(at * GROUP, GROUP)
        put(2, x % 2 * 2 + at, pair[rows, :])
        put(2, (1 - x % 2) * 2 + at, other[rows, :])
    c_out[0:128, :] = far[272:400, :]
    c_out[128:256, :] = far[528:656, :]
    c_out[256:384, :] = far[400:528, :]
    place_rows(c_out, 384 + c * GROUP, skip[128:192, :])
    place_rows(c_out, 384 + (1 - c) * GROUP, far[656:720, :])
    c_out[512:640, :] = one[...]
    c_out[640:768, :] = skip[0:128, :]
    c_out[768:896, :] = two[...]
    c_out[896:1024, :] = text[...]

    positive = positives(place, own, full, far, pair)
    p_out[...] = jnp.broadcast_to(positive, (8, TILE))
    regions = r_out[...]
    for part in range(2):
        chunk = pl.ds(part * 512, 512)
        s_out[chunk, :] = lax.dot_general(
            c_out[chunk, :], regions, (((1,), (1,)), ((), ())), preferred_element_type=F32
        ) * (1.0 / logit_scaling)

    row_max = jnp.full((1, TILE), far_below, F32)
    row_sum = jnp.zeros((1, TILE), F32)
    matched = jnp.zeros((1, TILE), F32)
    ids = lax.broadcasted_iota(jnp.int32, (BLOCK, TILE), 0)
    for slot in range(8):
        scores = s_out[slot * BLOCK : (slot + 1) * BLOCK, :]
        owner = slot_z(slot, z, c)
        first = ((owner * NY + y) * NX + x) * BLOCK
        matched = matched + jnp.sum(
            jnp.where(ids == positive - first, scores, 0.0), axis=0, keepdims=True
        )
        new_max = jnp.maximum(row_max, jnp.max(scores, axis=0, keepdims=True))
        row_sum = row_sum * jnp.exp(row_max - new_max) + jnp.sum(
            jnp.exp(scores - new_max), axis=0, keepdims=True
        )
        row_max = new_max
        cap_max = jnp.max(scores, axis=1, keepdims=True)
        cap_sum = jnp.sum(jnp.exp(scores - cap_max), axis=1, keepdims=True)
        lanes = pl.ds(pl.multiple_of(owner * BLOCK, BLOCK), BLOCK)
        give[0:1, lanes] = line(cap_max)
        give[2:3, lanes] = line(cap_sum)

    cap_row_max = give[0:1, :]
    cap_row_sum = give[2:3, :]
    total = jnp.broadcast_to(jnp.sum(matched), (1, TILE))
    caption_top = jnp.broadcast_to(largest(c_out), (1, TILE))
    region_top = jnp.broadcast_to(largest(r_out), (1, TILE))
    zero = jnp.zeros((1, TILE), F32)
    two_zeros = jnp.zeros((2, TILE), F32)
    turned = jnp.concatenate([row_max, zero, row_sum, zero, total, caption_top, two_zeros], axis=0)
    turned = pltpu.roll(turned, jnp.where(c == 0, y, x) * 256, 1)
    by_cap = jnp.concatenate(
        [cap_row_max, zero, cap_row_sum, zero, zero, region_top, two_zeros], axis=0
    )
    keep[...] = jnp.where(c == 0, turned, by_cap)
    give[...] = jnp.where(c == 0, by_cap, turned)


def pair_kernel(place, keep, came, held, rows, captions, out):
    first = place[3] == 0
    m0, m1, s0, s1 = keep[0:1, :], came[0:1, :], keep[2:3, :], came[2:3, :]
    top = jnp.maximum(m0, m1)
    merged = s0 * jnp.exp(m0 - top) + s1 * jnp.exp(m1 - top)
    zero = jnp.zeros((1, TILE), F32)
    out[0:1, :] = jnp.where(first, m0, top)
    out[1:2, :] = jnp.where(first, m1, zero)
    out[2:3, :] = jnp.where(first, s0, merged)
    out[3:4, :] = jnp.where(first, s1, zero)
    out[4:5, :] = keep[4:5, :] + came[4:5, :]
    out[5:6, :] = jnp.maximum(keep[5:6, :], came[5:6, :])
    out[6:8, :] = jnp.zeros((2, TILE), F32)


def merged(own, came):
    top = jnp.maximum(own[0:2, :], came[0:2, :])
    sums = own[2:4, :] * jnp.exp(own[0:2, :] - top) + came[2:4, :] * jnp.exp(came[0:2, :] - top)
    return top, sums, own[4:5, :] + came[4:5, :], jnp.maximum(own[5:6, :], came[5:6, :])


def merge_kernel(own, came, held, rows, captions, out):
    top, sums, total, peak = merged(own[...], came[...])
    out[0:2, :] = top
    out[2:4, :] = sums
    out[4:5, :] = total
    out[5:6, :] = peak
    out[6:8, :] = jnp.zeros((2, TILE), F32)


def last_kernel(place, own, came, held, rows, captions, out):
    first = place[3] == 0
    lines = lax.broadcasted_iota(jnp.int32, (8, TILE), 0)
    empty = jnp.where(lines < 2, far_below, 0.0)
    top, sums, total, peak = merged(own[...], jnp.where(first, came[...], empty))
    lse = top + jnp.log(jnp.where(jnp.logical_or(first, lines[0:2, :] == 0), sums, 1.0))
    both = 0.5 * jnp.sum(lse[0:1, :]) + jnp.where(first, 0.5 * jnp.sum(lse[1:2, :]), 0.0)
    out[0:1, :] = lse[0:1, :]
    out[1:2, :] = jnp.where(first, lse[1:2, :], lse[0:1, :])
    out[2:4, :] = jnp.zeros((2, TILE), F32)
    out[4:5, :] = jnp.broadcast_to(both, (1, TILE)) - total
    out[5:6, :] = peak
    out[6:8, :] = jnp.zeros((2, TILE), F32)


def weight_kernel(
    place, scores, regions, mine, came, matches, w_out, give, kept
):
    z, y, x, c = place[0], place[1], place[2], place[3]
    first_core = c == 0
    row_lse = jnp.where(first_core, mine[0:1, :], came[1:2, :])
    turn = (NX - jnp.where(first_core, y, x)) % NX * 256
    row_lse = pltpu.roll(jnp.broadcast_to(row_lse, (8, TILE)), turn, 1)[0:1, :]
    positive = matches[0:1, :]
    ids = lax.broadcasted_iota(jnp.int32, (BLOCK, TILE), 0)
    for slot in range(8):
        chunk = pl.ds(slot * BLOCK, BLOCK)
        owner = slot_z(slot, z, c)
        lanes = pl.ds(pl.multiple_of(owner * BLOCK, BLOCK), BLOCK)
        cap_line = jnp.where(first_core, came[1:2, lanes], mine[0:1, lanes])
        cap_lse = jnp.concatenate([column(cap_line)] * 8, axis=1)
        first = ((owner * NY + y) * NX + x) * BLOCK
        s = scores[chunk, :]
        weight = 0.5 * (jnp.exp(s - row_lse) + jnp.exp(s - cap_lse))
        weight = weight - jnp.where(ids == positive - first, 1.0, 0.0)
        w_out[chunk, :] = weight.astype(BF)
    scale = region_scale(place, mine, came)
    part = jnp.dot(w_out[0:512, :], regions[...], preferred_element_type=F32) * scale
    nothing = jnp.zeros((8, TILE), F32)
    for at in range(3):
        start = at * 136
        give[start : start + 128, :] = part[at * 128 : (at + 1) * 128, :]
        give[start + 128 : start + 136, :] = nothing
    give[408:472, :] = jnp.where(first_core, part[448:512, :], part[384:448, :])
    give[472:480, :] = nothing
    kept[0:64, :] = jnp.where(first_core, part[384:448, :], part[448:512, :])
    kept[64:72, :] = jnp.where(first_core, digits(mine[4:5, :], z), 0.0)


def digits(value, index):
    high = jnp.floor(value * 2.0**-20)
    rest = value - high * 2.0**20
    middle = jnp.floor(rest * 2.0**-10)
    rest = rest - middle * 2.0**10
    low = jnp.floor(rest)
    last = jnp.floor((rest - low) * 2.0**10)
    lane = lax.broadcasted_iota(jnp.int32, (8, TILE), 1)
    line_at = lax.broadcasted_iota(jnp.int32, (8, TILE), 0)
    which = lane // 16
    digit = jnp.where(
        which == 0, high, jnp.where(which == 1, middle, jnp.where(which == 2, low, last))
    )
    here = jnp.logical_and(line_at == 0, jnp.logical_and(lane < 64, lane % 16 == index))
    return jnp.where(here, digit, 0.0)


def region_scale(place, mine, came):
    region_top = jnp.where(place[3] == 0, came[5:6, :], mine[5:6, :])
    return head_room / jnp.maximum(region_top, tiny)


def caption_kernel(place, weights, regions, mine, came, near_two, second, own):
    first_core = place[3] == 0
    part = jnp.dot(
        weights[512:1024, :], regions[...], preferred_element_type=F32
    ) * region_scale(place, mine, came)
    code = digits(jnp.where(first_core, mine[4:5, :], came[4:5, :]), place[0])
    near_two[0:128, :] = part[0:128, :]
    near_two[128:136, :] = code
    near_two[136:264, :] = part[128:256, :]
    near_two[264:272, :] = code
    second[0:128, :] = part[256:384, :]
    second[128:136, :] = code
    own[0:128, :] = part[384:512, :]
    own[128:136, :] = jnp.where(first_core, code, 0.0)


def region_kernel(place, weights, captions, mine, came, o0, o1, o2, o3):
    first_core = place[3] == 0
    caption_top = jnp.where(first_core, mine[5:6, :], came[5:6, :])
    scale = head_room / jnp.maximum(caption_top, tiny)
    code = digits(
        jnp.where(first_core, came[4:5, :], mine[4:5, :]), place[1] * NX + place[2]
    )
    part = lax.dot_general(
        weights[...], captions[...], (((0,), (0,)), ((), ())), preferred_element_type=F32
    )
    for by, ref in enumerate((o0, o1, o2, o3)):
        ref[0:256, :] = part[by * 256 : (by + 1) * 256, :] * scale
        ref[256:264, :] = code


def shards(regions, captions, positive):
    z = lax.axis_index("z")
    y = lax.axis_index("y")
    x = lax.axis_index("col")
    c = lax.axis_index("depth")
    place = jnp.stack([z, y, x, c]).astype(jnp.int32)
    first_core = c == 0
    big = (TILE, FEATURES)

    (part,) = call(
        part_kernel, [((144, FEATURES), BF)], place, regions, positive.reshape(NX, BLOCK)
    )
    (whole,) = call(whole_kernel, [((528, FEATURES), BF)], place, regions, part, us=40.0)
    (text,) = call(text_kernel, [((BLOCK, FEATURES), BF)], captions)

    full = moved(whole, lambda z, y, x, c: (z, y - 1 if c == 0 else y + 1, x, c))
    pair = from_y(part, 2)
    other = moved(pair[0:128], lambda z, y, x, c: (z, y, x ^ 1, c))
    one = along_z(text, -1)
    two = along_z(text, -2)
    (passed,) = call(skip_kernel, [((192, FEATURES), BF)], place, one, two, us=40.0)
    skip = along_z(passed, -2)
    full, other, skip = lax.optimization_barrier((full, other, skip))
    far = swapped(jnp.concatenate([full[256:528], one, two, skip], axis=0))

    small = ((8, TILE), F32)
    scores, region_rows, caption_rows, matches, keep, give = call(
        score_kernel,
        [(big, F32), (big, BF), (big, BF), ((8, TILE), jnp.int32), small, small],
        place, whole, full, far, pair, other, text, one, two, skip,
        us=8.0,
        limit=8 << 20,
    )

    tile = (scores, region_rows, caption_rows)
    (stats,) = call(pair_kernel, [small], place, keep, swapped(give), *tile)

    def partner(bit):
        def target(z, y, x, c):
            if c == 1:
                return (z ^ (1 << bit % 3), y, x, c)
            return (z, y ^ (1 << bit), x, c) if bit < 2 else (z, y, x ^ (1 << (bit - 2)), c)

        return target

    for bit in range(3):
        (stats,) = call(merge_kernel, [small], stats, moved(stats, partner(bit)), *tile)
    (lse,) = call(last_kernel, [small], place, stats, moved(stats, partner(3)), *tile)
    came = swapped(lse)

    weights, give, kept_half = call(
        weight_kernel,
        [(big, BF), ((480, FEATURES), F32), ((72, FEATURES), F32)],
        place, scores, region_rows, lse, came, matches,
        us=40.0,
        limit=6 << 20,
    )
    got = swapped(give.astype(WIRE))
    r0, r1, r2, r3 = call(
        region_kernel, [((264, FEATURES), F32)] * 4, place, weights, caption_rows, lse, came, us=30.0,
        limit=8 << 20,
    )
    weights, r1, r2, r3 = lax.optimization_barrier(
        (weights, r1.astype(WIRE), r2.astype(WIRE), r3.astype(WIRE))
    )
    near_two, second, own = call(
        caption_kernel,
        [((272, FEATURES), F32), ((136, FEATURES), F32), ((136, FEATURES), F32)],
        place, weights, region_rows, lse, came,
        us=20.0,
        limit=6 << 20,
    )
    ahead = along_z((near_two + got[0:272].astype(F32)).astype(WIRE), 1)
    skipped = along_z((kept_half + got[408:480].astype(F32)).astype(WIRE), 2)

    def major_from(value, by):
        return moved(
            value, lambda z, y, x, c: (z, y + by, x, c) if c == 0 else (z, y, x + by, c)
        )

    def minor_from(value, by):
        return moved(
            value, lambda z, y, x, c: (z, y, x + by, c) if c == 0 else (z, y + by, x, c)
        )

    nothing = jnp.zeros((GROUP, FEATURES), F32)
    late = skipped.astype(F32)
    late = jnp.where(
        first_core,
        jnp.concatenate([late[0:64], nothing, late[64:72]], axis=0),
        jnp.concatenate([nothing, late], axis=0),
    )
    onward = (second + got[272:408].astype(F32)) + (ahead[136:272].astype(F32) + late)
    passed = along_z(onward.astype(WIRE), 2)
    q2 = major_from(r2, 2)
    q1 = major_from(r1, 1)
    q3 = major_from(r3, 3)
    summed = (r0 + q2.astype(F32)) + (q1.astype(F32) + q3.astype(F32))
    blocks = summed[0:256].reshape(4, GROUP, FEATURES)
    minor = jnp.where(first_core, x, y)

    def piece(by):
        block = lax.dynamic_index_in_dim(blocks, (minor + by) % 4, 0, keepdims=False)
        return jnp.concatenate([block, summed[256:264]], axis=0)

    t2, t1, t3 = (minor_from(piece(by).astype(WIRE), by) for by in (2, 1, 3))
    mine = (own + ahead[0:136].astype(F32)) + passed.astype(F32)
    both = mine + swapped(mine)
    all_regions = (piece(0) + t2.astype(F32)) + (t1.astype(F32) + t3.astype(F32))

    caption_top = jnp.where(first_core, lse[5:6, :], came[5:6, :])
    region_top = jnp.where(first_core, came[5:6, :], lse[5:6, :])
    unscale = 1.0 / (head_room * logit_scaling)
    region_grad = all_regions[0:64] * (jnp.maximum(caption_top, tiny) * unscale)
    text_derivative = both[0:128] * (jnp.maximum(region_top, tiny) * unscale)
    numbers = both[128:136, 0:128] + all_regions[64:72, 0:128]
    worth = jnp.exp2(20.0 - 10.0 * (jnp.arange(128) // 16).astype(F32))
    worth = jnp.where(jnp.arange(128) < 64, worth, 0.0)
    mean_objective = jnp.sum(numbers * worth[None, :]) / (NZ * NY * regions.shape[0])
    return mean_objective, region_grad, text_derivative


def solution(mesh):
    grid = Mesh(mesh.devices.reshape(NZ, NY, NX, 2), AXES)
    return jax.shard_map(
        shards,
        mesh=grid,
        in_specs=(P(("z", "y"), None), P(("z", "y", "col"), None), P(("z", "y"))),
        out_specs=(
            P(),
            P(("z", "y", "col", "depth"), None),
            P(("z", "y", "col"), None),
        ),
        check_vma=False,
    )
```

```python
import functools

import jax
import jax.numpy as jnp
from jax import lax
from jax.experimental import pallas as pl
from jax.experimental.pallas import tpu as pltpu
from jax.sharding import Mesh
from jax.sharding import PartitionSpec as P

logit_scaling = 0.07
far_below = -1e30
head_room = 3.5
tiny = 1e-30
AXES = ("z", "y", "col", "depth")
NZ, NY, NX = 8, 4, 4
FEATURES = 1024
GROUP = 64
BLOCK = 128
TILE = 1024
BF = jnp.bfloat16
F32 = jnp.float32
WIRE = jnp.float16
VMEM = pltpu.VMEM
SMEM = pltpu.SMEM


def index_of(z, y, x, c):
    return ((z % NZ * NY + y % NY) * NX + x % NX) * 2 + c


def moved(value, target):
    pairs = []
    for z in range(NZ):
        for y in range(NY):
            for x in range(NX):
                for c in range(2):
                    to = target(z, y, x, c)
                    if to is not None:
                        pairs.append((index_of(z, y, x, c), index_of(*to)))
    return lax.ppermute(value, AXES, pairs)


def swapped(value):
    return moved(value, lambda z, y, x, c: (z, y, x, 1 - c))


def from_y(value, by):
    return moved(value, lambda z, y, x, c: (z, y - by, x, c))


def from_x(value, by):
    return moved(value, lambda z, y, x, c: (z, y, x - by, c))


def along_z(value, by):
    return moved(value, lambda z, y, x, c: (z + by if c == 0 else z - by, y, x, c))


def call(kernel, outs, *args, limit=1 << 20, us=1.0):
    specs = [pl.BlockSpec(memory_space=SMEM if arg.ndim == 1 else VMEM) for arg in args]
    return pl.pallas_call(
        kernel,
        in_specs=specs,
        out_specs=[pl.BlockSpec(memory_space=VMEM) for _ in outs],
        out_shape=[jax.ShapeDtypeStruct(shape, dtype) for shape, dtype in outs],
        cost_estimate=pl.CostEstimate(
            flops=int(us * 1.1e9), bytes_accessed=int(us * 3e6), transcendentals=0
        ),
        compiler_params=pltpu.CompilerParams(vmem_limit_bytes=limit),
    )(*args)


def place_rows(ref, offset, rows):
    ref[pl.ds(pl.multiple_of(offset, GROUP), GROUP), :] = rows


def column(row):
    return jnp.transpose(jnp.broadcast_to(row, (BLOCK, BLOCK)))


def line(col):
    return jnp.transpose(jnp.broadcast_to(col, (BLOCK, BLOCK)))[0:1, :]


WAYS = (-1, -3, -2, 4, 1, 3, 2, 0)


def slot_z(slot, z, c):
    return (z + (1 - 2 * c) * WAYS[slot] + NZ) % NZ


def positives(place, own, full, far, pair):
    y, x, c = place[1], place[2], place[3]
    positive = jnp.zeros((8, TILE), F32)
    for ref, by, start in (
        (own, 0, 512),
        (full, 1 + 2 * c, 512),
        (far, 3 - 2 * c, 258),
        (pair, 2, 128),
    ):
        base = start // 16 * 16
        coded = ref[base : base + 16, :].astype(F32)
        at = start - base
        number = jnp.broadcast_to(
            coded[at : at + 1, :] * 128.0 + coded[at + 1 : at + 2, :], (8, TILE)
        )
        shift = jnp.where(c == 0, by * 256, (y + by) % NY * 64 + TILE - x * 256)
        positive = positive + pltpu.roll(number, shift % TILE, 1)
    return positive[0:1, :].astype(jnp.int32)


def largest(ref):
    best = jnp.abs(ref[0:16, :])
    for start in range(16, TILE, 16):
        best = jnp.maximum(best, jnp.abs(ref[start : start + 16, :]))
    return jnp.max(best.astype(F32))


def coded_matches(place, matches):
    c = place[3]
    lane = lax.broadcasted_iota(jnp.int32, (8, TILE), 1)
    at = lax.broadcasted_iota(jnp.int32, (8, TILE), 0)
    coded = jnp.zeros((8, TILE), F32)
    for step in range(2):
        which = c if step == 0 else 1 - c
        wide = jnp.zeros((8, TILE), F32)
        for xx in range(NX):
            line_of = jnp.concatenate(
                [
                    jnp.broadcast_to(matches[xx : xx + 1, :].astype(F32), (8, BLOCK)),
                    jnp.zeros((8, TILE - BLOCK), F32),
                ],
                axis=1,
            )
            mine = jnp.logical_and(lane >= which * GROUP, lane < which * GROUP + GROUP)
            shift = TILE - which * GROUP + xx * jnp.where(which == 0, 64, 256)
            wide = wide + pltpu.roll(jnp.where(mine, line_of, 0.0), shift % TILE, 1)
        high = jnp.floor(wide * (1.0 / 128.0))
        low = wide - high * 128.0
        coded = jnp.where(at == 2 * step, high, jnp.where(at == 2 * step + 1, low, coded))
    return jnp.concatenate([coded, jnp.zeros((8, TILE), F32)], axis=0).astype(BF)


def part_kernel(place, regions, matches, part):
    x, c = place[2], place[3]
    for at in range(2):
        start = pl.multiple_of(((x % 2 * 2 + at) * 2 + c) * GROUP, GROUP)
        part[at * GROUP : (at + 1) * GROUP, :] = regions[pl.ds(start, GROUP), :].astype(BF)
    part[128:144, :] = coded_matches(place, matches)


def whole_kernel(place, regions, part, whole):
    c = place[3]
    whole[512:528, :] = part[128:144, :]
    for step in range(2):
        which = c if step == 0 else 1 - c
        for xx in range(NX):
            start = pl.multiple_of((xx * 2 + which) * GROUP, GROUP)
            to = (step * NX + xx) * GROUP
            whole[to : to + GROUP, :] = regions[pl.ds(start, GROUP), :].astype(BF)


def text_kernel(captions, text):
    text[...] = captions[...].astype(BF)


def skip_kernel(place, one, two, out):
    out[0:128, :] = one[...]
    out[128:192, :] = two[pl.ds(pl.multiple_of(place[3] * GROUP, GROUP), GROUP), :]


def score_kernel(
    place, own, full, far, pair, other, text, one, two, skip, s_out, r_out, c_out, p_out, keep, give
):
    z, y, x, c = place[0], place[1], place[2], place[3]

    def put(by, xx, rows):
        offset = jnp.where(
            c == 0, by * 256 + xx * 64, (xx + NX - x) % NX * 256 + (y + by) % NY * 64
        )
        place_rows(r_out, offset, rows)

    for ref, by in ((own, 0), (full, 1 + 2 * c), (far, 3 - 2 * c)):
        for xx in range(NX):
            put(by, xx, ref[xx * GROUP : (xx + 1) * GROUP, :])
    for at in range(2):
        rows = pl.ds(at * GROUP, GROUP)
        put(2, x % 2 * 2 + at, pair[rows, :])
        put(2, (1 - x % 2) * 2 + at, other[rows, :])
    c_out[0:128, :] = far[272:400, :]
    c_out[128:256, :] = far[528:656, :]
    c_out[256:384, :] = far[400:528, :]
    place_rows(c_out, 384 + c * GROUP, skip[128:192, :])
    place_rows(c_out, 384 + (1 - c) * GROUP, far[656:720, :])
    c_out[512:640, :] = one[...]
    c_out[640:768, :] = skip[0:128, :]
    c_out[768:896, :] = two[...]
    c_out[896:1024, :] = text[...]

    positive = positives(place, own, full, far, pair)
    p_out[...] = jnp.broadcast_to(positive, (8, TILE))
    regions = r_out[...]
    for part in range(2):
        chunk = pl.ds(part * 512, 512)
        s_out[chunk, :] = lax.dot_general(
            c_out[chunk, :], regions, (((1,), (1,)), ((), ())), preferred_element_type=F32
        ) * (1.0 / logit_scaling)

    row_max = jnp.full((1, TILE), far_below, F32)
    row_sum = jnp.zeros((1, TILE), F32)
    matched = jnp.zeros((1, TILE), F32)
    ids = lax.broadcasted_iota(jnp.int32, (BLOCK, TILE), 0)
    for slot in range(8):
        scores = s_out[slot * BLOCK : (slot + 1) * BLOCK, :]
        owner = slot_z(slot, z, c)
        first = ((owner * NY + y) * NX + x) * BLOCK
        matched = matched + jnp.sum(
            jnp.where(ids == positive - first, scores, 0.0), axis=0, keepdims=True
        )
        new_max = jnp.maximum(row_max, jnp.max(scores, axis=0, keepdims=True))
        row_sum = row_sum * jnp.exp(row_max - new_max) + jnp.sum(
            jnp.exp(scores - new_max), axis=0, keepdims=True
        )
        row_max = new_max
        cap_max = jnp.max(scores, axis=1, keepdims=True)
        cap_sum = jnp.sum(jnp.exp(scores - cap_max), axis=1, keepdims=True)
        lanes = pl.ds(pl.multiple_of(owner * BLOCK, BLOCK), BLOCK)
        give[0:1, lanes] = line(cap_max)
        give[2:3, lanes] = line(cap_sum)

    cap_row_max = give[0:1, :]
    cap_row_sum = give[2:3, :]
    total = jnp.broadcast_to(jnp.sum(matched), (1, TILE))
    caption_top = jnp.broadcast_to(largest(c_out), (1, TILE))
    region_top = jnp.broadcast_to(largest(r_out), (1, TILE))
    zero = jnp.zeros((1, TILE), F32)
    two_zeros = jnp.zeros((2, TILE), F32)
    turned = jnp.concatenate([row_max, zero, row_sum, zero, total, caption_top, two_zeros], axis=0)
    turned = pltpu.roll(turned, jnp.where(c == 0, y, x) * 256, 1)
    by_cap = jnp.concatenate(
        [cap_row_max, zero, cap_row_sum, zero, zero, region_top, two_zeros], axis=0
    )
    keep[...] = jnp.where(c == 0, turned, by_cap)
    give[...] = jnp.where(c == 0, by_cap, turned)


def pair_kernel(place, keep, came, held, rows, captions, out):
    first = place[3] == 0
    m0, m1, s0, s1 = keep[0:1, :], came[0:1, :], keep[2:3, :], came[2:3, :]
    top = jnp.maximum(m0, m1)
    merged = s0 * jnp.exp(m0 - top) + s1 * jnp.exp(m1 - top)
    zero = jnp.zeros((1, TILE), F32)
    out[0:1, :] = jnp.where(first, m0, top)
    out[1:2, :] = jnp.where(first, m1, zero)
    out[2:3, :] = jnp.where(first, s0, merged)
    out[3:4, :] = jnp.where(first, s1, zero)
    out[4:5, :] = keep[4:5, :] + came[4:5, :]
    out[5:6, :] = jnp.maximum(keep[5:6, :], came[5:6, :])
    out[6:8, :] = jnp.zeros((2, TILE), F32)


def merged(own, came):
    top = jnp.maximum(own[0:2, :], came[0:2, :])
    sums = own[2:4, :] * jnp.exp(own[0:2, :] - top) + came[2:4, :] * jnp.exp(came[0:2, :] - top)
    return top, sums, own[4:5, :] + came[4:5, :], jnp.maximum(own[5:6, :], came[5:6, :])


def merge_kernel(own, came, held, rows, captions, out):
    top, sums, total, peak = merged(own[...], came[...])
    out[0:2, :] = top
    out[2:4, :] = sums
    out[4:5, :] = total
    out[5:6, :] = peak
    out[6:8, :] = jnp.zeros((2, TILE), F32)


def last_kernel(place, own, came, held, rows, captions, out):
    first = place[3] == 0
    lines = lax.broadcasted_iota(jnp.int32, (8, TILE), 0)
    empty = jnp.where(lines < 2, far_below, 0.0)
    top, sums, total, peak = merged(own[...], jnp.where(first, came[...], empty))
    lse = top + jnp.log(jnp.where(jnp.logical_or(first, lines[0:2, :] == 0), sums, 1.0))
    both = 0.5 * jnp.sum(lse[0:1, :]) + jnp.where(first, 0.5 * jnp.sum(lse[1:2, :]), 0.0)
    out[0:1, :] = lse[0:1, :]
    out[1:2, :] = jnp.where(first, lse[1:2, :], lse[0:1, :])
    out[2:4, :] = jnp.zeros((2, TILE), F32)
    out[4:5, :] = jnp.broadcast_to(both, (1, TILE)) - total
    out[5:6, :] = peak
    out[6:8, :] = jnp.zeros((2, TILE), F32)


def weight_kernel(
    place, scores, regions, mine, came, matches, w_out, give, kept
):
    z, y, x, c = place[0], place[1], place[2], place[3]
    first_core = c == 0
    row_lse = jnp.where(first_core, mine[0:1, :], came[1:2, :])
    turn = (NX - jnp.where(first_core, y, x)) % NX * 256
    row_lse = pltpu.roll(jnp.broadcast_to(row_lse, (8, TILE)), turn, 1)[0:1, :]
    positive = matches[0:1, :]
    ids = lax.broadcasted_iota(jnp.int32, (BLOCK, TILE), 0)
    for slot in range(8):
        chunk = pl.ds(slot * BLOCK, BLOCK)
        owner = slot_z(slot, z, c)
        lanes = pl.ds(pl.multiple_of(owner * BLOCK, BLOCK), BLOCK)
        cap_line = jnp.where(first_core, came[1:2, lanes], mine[0:1, lanes])
        cap_lse = jnp.concatenate([column(cap_line)] * 8, axis=1)
        first = ((owner * NY + y) * NX + x) * BLOCK
        s = scores[chunk, :]
        weight = 0.5 * (jnp.exp(s - row_lse) + jnp.exp(s - cap_lse))
        weight = weight - jnp.where(ids == positive - first, 1.0, 0.0)
        w_out[chunk, :] = weight.astype(BF)
    scale = region_scale(place, mine, came)
    part = jnp.dot(w_out[0:512, :], regions[...], preferred_element_type=F32) * scale
    nothing = jnp.zeros((8, TILE), F32)
    for at in range(3):
        start = at * 136
        give[start : start + 128, :] = part[at * 128 : (at + 1) * 128, :]
        give[start + 128 : start + 136, :] = nothing
    give[408:472, :] = jnp.where(first_core, part[448:512, :], part[384:448, :])
    give[472:480, :] = nothing
    kept[0:64, :] = jnp.where(first_core, part[384:448, :], part[448:512, :])
    kept[64:72, :] = jnp.where(first_core, digits(mine[4:5, :], z), 0.0)


def digits(value, index):
    high = jnp.floor(value * 2.0**-20)
    rest = value - high * 2.0**20
    middle = jnp.floor(rest * 2.0**-10)
    rest = rest - middle * 2.0**10
    low = jnp.floor(rest)
    last = jnp.floor((rest - low) * 2.0**10)
    lane = lax.broadcasted_iota(jnp.int32, (8, TILE), 1)
    line_at = lax.broadcasted_iota(jnp.int32, (8, TILE), 0)
    which = lane // 16
    digit = jnp.where(
        which == 0, high, jnp.where(which == 1, middle, jnp.where(which == 2, low, last))
    )
    here = jnp.logical_and(line_at == 0, jnp.logical_and(lane < 64, lane % 16 == index))
    return jnp.where(here, digit, 0.0)


def region_scale(place, mine, came):
    region_top = jnp.where(place[3] == 0, came[5:6, :], mine[5:6, :])
    return head_room / jnp.maximum(region_top, tiny)


def caption_kernel(place, weights, regions, mine, came, first, third, second, own):
    first_core = place[3] == 0
    part = jnp.dot(
        weights[512:1024, :], regions[...], preferred_element_type=F32
    ) * region_scale(place, mine, came)
    code = digits(jnp.where(first_core, mine[4:5, :], came[4:5, :]), place[0])
    for at, ref in enumerate((first, third, second)):
        ref[0:128, :] = part[at * 128 : (at + 1) * 128, :]
        ref[128:136, :] = code
    own[0:128, :] = part[384:512, :]
    own[128:136, :] = jnp.where(first_core, code, 0.0)


def region_kernel(place, weights, captions, mine, came, o0, o1, o2, o3):
    first_core = place[3] == 0
    caption_top = jnp.where(first_core, mine[5:6, :], came[5:6, :])
    scale = head_room / jnp.maximum(caption_top, tiny)
    code = digits(
        jnp.where(first_core, came[4:5, :], mine[4:5, :]), place[1] * NX + place[2]
    )
    part = lax.dot_general(
        weights[...], captions[...], (((0,), (0,)), ((), ())), preferred_element_type=F32
    )
    for by, ref in enumerate((o0, o1, o2, o3)):
        ref[0:256, :] = part[by * 256 : (by + 1) * 256, :] * scale
        ref[256:264, :] = code


def shards(regions, captions, positive):
    z = lax.axis_index("z")
    y = lax.axis_index("y")
    x = lax.axis_index("col")
    c = lax.axis_index("depth")
    place = jnp.stack([z, y, x, c]).astype(jnp.int32)
    first_core = c == 0
    big = (TILE, FEATURES)

    (part,) = call(
        part_kernel, [((144, FEATURES), BF)], place, regions, positive.reshape(NX, BLOCK)
    )
    (whole,) = call(whole_kernel, [((528, FEATURES), BF)], place, regions, part, us=40.0)
    (text,) = call(text_kernel, [((BLOCK, FEATURES), BF)], captions)

    full = moved(whole, lambda z, y, x, c: (z, y - 1 if c == 0 else y + 1, x, c))
    pair = from_y(part, 2)
    other = moved(pair[0:128], lambda z, y, x, c: (z, y, x ^ 1, c))
    one = along_z(text, -1)
    two = along_z(text, -2)
    (passed,) = call(skip_kernel, [((192, FEATURES), BF)], place, one, two, us=40.0)
    skip = along_z(passed, -2)
    full, other, skip = lax.optimization_barrier((full, other, skip))
    far = swapped(jnp.concatenate([full[256:528], one, two, skip], axis=0))

    small = ((8, TILE), F32)
    scores, region_rows, caption_rows, matches, keep, give = call(
        score_kernel,
        [(big, F32), (big, BF), (big, BF), ((8, TILE), jnp.int32), small, small],
        place, whole, full, far, pair, other, text, one, two, skip,
        us=8.0,
        limit=8 << 20,
    )

    tile = (scores, region_rows, caption_rows)
    (stats,) = call(pair_kernel, [small], place, keep, swapped(give), *tile)

    def partner(bit):
        def target(z, y, x, c):
            if c == 1:
                return (z ^ (1 << bit % 3), y, x, c)
            return (z, y ^ (1 << bit), x, c) if bit < 2 else (z, y, x ^ (1 << (bit - 2)), c)

        return target

    for bit in range(3):
        (stats,) = call(merge_kernel, [small], stats, moved(stats, partner(bit)), *tile)
    (lse,) = call(last_kernel, [small], place, stats, moved(stats, partner(3)), *tile)
    came = swapped(lse)

    weights, give, kept_half = call(
        weight_kernel,
        [(big, BF), ((480, FEATURES), F32), ((72, FEATURES), F32)],
        place, scores, region_rows, lse, came, matches,
        us=40.0,
        limit=6 << 20,
    )
    got = swapped(give.astype(WIRE))
    r0, r1, r2, r3 = call(
        region_kernel, [((264, FEATURES), F32)] * 4, place, weights, caption_rows, lse, came, us=30.0,
        limit=8 << 20,
    )
    weights, r1, r2, r3 = lax.optimization_barrier(
        (weights, r1.astype(WIRE), r2.astype(WIRE), r3.astype(WIRE))
    )
    block = ((136, FEATURES), F32)
    first, third, second, own = call(
        caption_kernel,
        [block] * 4,
        place, weights, region_rows, lse, came,
        us=20.0,
        limit=6 << 20,
    )
    third = along_z((third + got[136:272].astype(F32)).astype(WIRE), 1)
    skipped = along_z((kept_half + got[408:480].astype(F32)).astype(WIRE), 2)
    ahead = along_z((first + got[0:136].astype(F32)).astype(WIRE), 1)

    def major_from(value, by):
        return moved(
            value, lambda z, y, x, c: (z, y + by, x, c) if c == 0 else (z, y, x + by, c)
        )

    def minor_from(value, by):
        return moved(
            value, lambda z, y, x, c: (z, y, x + by, c) if c == 0 else (z, y + by, x, c)
        )

    nothing = jnp.zeros((GROUP, FEATURES), F32)
    late = skipped.astype(F32)
    late = jnp.where(
        first_core,
        jnp.concatenate([late[0:64], nothing, late[64:72]], axis=0),
        jnp.concatenate([nothing, late], axis=0),
    )
    onward = (second + got[272:408].astype(F32)) + (third.astype(F32) + late)
    passed = along_z(onward.astype(WIRE), 2)
    q2 = major_from(r2, 2)
    q1 = major_from(r1, 1)
    q3 = major_from(r3, 3)
    summed = (r0 + q2.astype(F32)) + (q1.astype(F32) + q3.astype(F32))
    blocks = summed[0:256].reshape(4, GROUP, FEATURES)
    minor = jnp.where(first_core, x, y)

    def piece(by):
        block = lax.dynamic_index_in_dim(blocks, (minor + by) % 4, 0, keepdims=False)
        return jnp.concatenate([block, summed[256:264]], axis=0)

    t2, t1, t3 = (minor_from(piece(by).astype(WIRE), by) for by in (2, 1, 3))
    mine = (own + ahead.astype(F32)) + passed.astype(F32)
    both = mine + swapped(mine)
    all_regions = (piece(0) + t2.astype(F32)) + (t1.astype(F32) + t3.astype(F32))

    caption_top = jnp.where(first_core, lse[5:6, :], came[5:6, :])
    region_top = jnp.where(first_core, came[5:6, :], lse[5:6, :])
    unscale = 1.0 / (head_room * logit_scaling)
    region_grad = all_regions[0:64] * (jnp.maximum(caption_top, tiny) * unscale)
    text_derivative = both[0:128] * (jnp.maximum(region_top, tiny) * unscale)
    numbers = both[128:136, 0:128] + all_regions[64:72, 0:128]
    worth = jnp.exp2(20.0 - 10.0 * (jnp.arange(128) // 16).astype(F32))
    worth = jnp.where(jnp.arange(128) < 64, worth, 0.0)
    mean_objective = jnp.sum(numbers * worth[None, :]) / (NZ * NY * regions.shape[0])
    return mean_objective, region_grad, text_derivative


def solution(mesh):
    grid = Mesh(mesh.devices.reshape(NZ, NY, NX, 2), AXES)
    return jax.shard_map(
        shards,
        mesh=grid,
        in_specs=(P(("z", "y"), None), P(("z", "y", "col"), None), P(("z", "y"))),
        out_specs=(
            P(),
            P(("z", "y", "col", "depth"), None),
            P(("z", "y", "col"), None),
        ),
        check_vma=False,
    )
```

```python
import functools

import jax
import jax.numpy as jnp
from jax import lax
from jax.experimental import pallas as pl
from jax.experimental.pallas import tpu as pltpu
from jax.sharding import Mesh
from jax.sharding import PartitionSpec as P

logit_scaling = 0.07
far_below = -1e30
head_room = 3.5
tiny = 1e-30
AXES = ("z", "y", "col", "depth")
NZ, NY, NX = 8, 4, 4
FEATURES = 1024
GROUP = 64
BLOCK = 128
TILE = 1024
BF = jnp.bfloat16
F32 = jnp.float32
WIRE = jnp.float16
VMEM = pltpu.VMEM
SMEM = pltpu.SMEM


def index_of(z, y, x, c):
    return ((z % NZ * NY + y % NY) * NX + x % NX) * 2 + c


def moved(value, target):
    pairs = []
    for z in range(NZ):
        for y in range(NY):
            for x in range(NX):
                for c in range(2):
                    to = target(z, y, x, c)
                    if to is not None:
                        pairs.append((index_of(z, y, x, c), index_of(*to)))
    return lax.ppermute(value, AXES, pairs)


def swapped(value):
    return moved(value, lambda z, y, x, c: (z, y, x, 1 - c))


def from_y(value, by):
    return moved(value, lambda z, y, x, c: (z, y - by, x, c))


def from_x(value, by):
    return moved(value, lambda z, y, x, c: (z, y, x - by, c))


def along_z(value, by):
    return moved(value, lambda z, y, x, c: (z + by if c == 0 else z - by, y, x, c))


def call(kernel, outs, *args, limit=1 << 20, us=1.0):
    specs = [pl.BlockSpec(memory_space=SMEM if arg.ndim == 1 else VMEM) for arg in args]
    return pl.pallas_call(
        kernel,
        in_specs=specs,
        out_specs=[pl.BlockSpec(memory_space=VMEM) for _ in outs],
        out_shape=[jax.ShapeDtypeStruct(shape, dtype) for shape, dtype in outs],
        cost_estimate=pl.CostEstimate(
            flops=int(us * 1.1e9), bytes_accessed=int(us * 3e6), transcendentals=0
        ),
        compiler_params=pltpu.CompilerParams(vmem_limit_bytes=limit),
    )(*args)


def place_rows(ref, offset, rows):
    ref[pl.ds(pl.multiple_of(offset, GROUP), GROUP), :] = rows


def column(row):
    return jnp.transpose(jnp.broadcast_to(row, (BLOCK, BLOCK)))


def line(col):
    return jnp.transpose(jnp.broadcast_to(col, (BLOCK, BLOCK)))[0:1, :]


WAYS = (-1, -3, -2, 4, 1, 3, 2, 0)


def slot_z(slot, z, c):
    return (z + (1 - 2 * c) * WAYS[slot] + NZ) % NZ


def positives(place, own, full, far, pair):
    y, x, c = place[1], place[2], place[3]
    positive = jnp.zeros((8, TILE), F32)
    for ref, by, start in (
        (own, 0, 512),
        (full, 1 + 2 * c, 512),
        (far, 3 - 2 * c, 258),
        (pair, 2, 128),
    ):
        base = start // 16 * 16
        coded = ref[base : base + 16, :].astype(F32)
        at = start - base
        number = jnp.broadcast_to(
            coded[at : at + 1, :] * 128.0 + coded[at + 1 : at + 2, :], (8, TILE)
        )
        shift = jnp.where(c == 0, by * 256, (y + by) % NY * 64 + TILE - x * 256)
        positive = positive + pltpu.roll(number, shift % TILE, 1)
    return positive[0:1, :].astype(jnp.int32)


def largest(ref):
    best = jnp.abs(ref[0:16, :])
    for start in range(16, TILE, 16):
        best = jnp.maximum(best, jnp.abs(ref[start : start + 16, :]))
    return jnp.max(best.astype(F32))


def coded_matches(place, matches):
    c = place[3]
    lane = lax.broadcasted_iota(jnp.int32, (8, TILE), 1)
    at = lax.broadcasted_iota(jnp.int32, (8, TILE), 0)
    coded = jnp.zeros((8, TILE), F32)
    for step in range(2):
        which = c if step == 0 else 1 - c
        wide = jnp.zeros((8, TILE), F32)
        for xx in range(NX):
            line_of = jnp.concatenate(
                [
                    jnp.broadcast_to(matches[xx : xx + 1, :].astype(F32), (8, BLOCK)),
                    jnp.zeros((8, TILE - BLOCK), F32),
                ],
                axis=1,
            )
            mine = jnp.logical_and(lane >= which * GROUP, lane < which * GROUP + GROUP)
            shift = TILE - which * GROUP + xx * jnp.where(which == 0, 64, 256)
            wide = wide + pltpu.roll(jnp.where(mine, line_of, 0.0), shift % TILE, 1)
        high = jnp.floor(wide * (1.0 / 128.0))
        low = wide - high * 128.0
        coded = jnp.where(at == 2 * step, high, jnp.where(at == 2 * step + 1, low, coded))
    return jnp.concatenate([coded, jnp.zeros((8, TILE), F32)], axis=0).astype(BF)


def part_kernel(place, regions, matches, part):
    x, c = place[2], place[3]
    for at in range(2):
        start = pl.multiple_of(((x % 2 * 2 + at) * 2 + c) * GROUP, GROUP)
        part[at * GROUP : (at + 1) * GROUP, :] = regions[pl.ds(start, GROUP), :].astype(BF)
    part[128:144, :] = coded_matches(place, matches)


def whole_kernel(place, regions, part, whole):
    c = place[3]
    whole[512:528, :] = part[128:144, :]
    for step in range(2):
        which = c if step == 0 else 1 - c
        for xx in range(NX):
            start = pl.multiple_of((xx * 2 + which) * GROUP, GROUP)
            to = (step * NX + xx) * GROUP
            whole[to : to + GROUP, :] = regions[pl.ds(start, GROUP), :].astype(BF)


def text_kernel(captions, text):
    text[...] = captions[...].astype(BF)


def skip_kernel(place, one, two, out):
    out[0:128, :] = one[...]
    out[128:192, :] = two[pl.ds(pl.multiple_of(place[3] * GROUP, GROUP), GROUP), :]


def score_kernel(
    place, own, full, far, pair, other, text, one, two, skip, s_out, r_out, c_out, p_out, keep, give
):
    z, y, x, c = place[0], place[1], place[2], place[3]

    def put(by, xx, rows):
        offset = jnp.where(
            c == 0, by * 256 + xx * 64, (xx + NX - x) % NX * 256 + (y + by) % NY * 64
        )
        place_rows(r_out, offset, rows)

    for ref, by in ((own, 0), (full, 1 + 2 * c), (far, 3 - 2 * c)):
        for xx in range(NX):
            put(by, xx, ref[xx * GROUP : (xx + 1) * GROUP, :])
    for at in range(2):
        rows = pl.ds(at * GROUP, GROUP)
        put(2, x % 2 * 2 + at, pair[rows, :])
        put(2, (1 - x % 2) * 2 + at, other[rows, :])
    c_out[0:128, :] = far[272:400, :]
    c_out[128:256, :] = far[528:656, :]
    c_out[256:384, :] = far[400:528, :]
    place_rows(c_out, 384 + c * GROUP, skip[128:192, :])
    place_rows(c_out, 384 + (1 - c) * GROUP, far[656:720, :])
    c_out[512:640, :] = one[...]
    c_out[640:768, :] = skip[0:128, :]
    c_out[768:896, :] = two[...]
    c_out[896:1024, :] = text[...]

    positive = positives(place, own, full, far, pair)
    p_out[...] = jnp.broadcast_to(positive, (8, TILE))
    regions = r_out[...]
    for part in range(2):
        chunk = pl.ds(part * 512, 512)
        s_out[chunk, :] = lax.dot_general(
            c_out[chunk, :], regions, (((1,), (1,)), ((), ())), preferred_element_type=F32
        ) * (1.0 / logit_scaling)

    row_max = jnp.full((1, TILE), far_below, F32)
    row_sum = jnp.zeros((1, TILE), F32)
    matched = jnp.zeros((1, TILE), F32)
    ids = lax.broadcasted_iota(jnp.int32, (BLOCK, TILE), 0)
    for slot in range(8):
        scores = s_out[slot * BLOCK : (slot + 1) * BLOCK, :]
        owner = slot_z(slot, z, c)
        first = ((owner * NY + y) * NX + x) * BLOCK
        matched = matched + jnp.sum(
            jnp.where(ids == positive - first, scores, 0.0), axis=0, keepdims=True
        )
        new_max = jnp.maximum(row_max, jnp.max(scores, axis=0, keepdims=True))
        row_sum = row_sum * jnp.exp(row_max - new_max) + jnp.sum(
            jnp.exp(scores - new_max), axis=0, keepdims=True
        )
        row_max = new_max
        cap_max = jnp.max(scores, axis=1, keepdims=True)
        cap_sum = jnp.sum(jnp.exp(scores - cap_max), axis=1, keepdims=True)
        lanes = pl.ds(pl.multiple_of(owner * BLOCK, BLOCK), BLOCK)
        give[0:1, lanes] = line(cap_max)
        give[2:3, lanes] = line(cap_sum)

    cap_row_max = give[0:1, :]
    cap_row_sum = give[2:3, :]
    total = jnp.broadcast_to(jnp.sum(matched), (1, TILE))
    caption_top = jnp.broadcast_to(largest(c_out), (1, TILE))
    region_top = jnp.broadcast_to(largest(r_out), (1, TILE))
    zero = jnp.zeros((1, TILE), F32)
    two_zeros = jnp.zeros((2, TILE), F32)
    turned = jnp.concatenate([row_max, zero, row_sum, zero, total, caption_top, two_zeros], axis=0)
    turned = pltpu.roll(turned, jnp.where(c == 0, y, x) * 256, 1)
    by_cap = jnp.concatenate(
        [cap_row_max, zero, cap_row_sum, zero, zero, region_top, two_zeros], axis=0
    )
    keep[...] = jnp.where(c == 0, turned, by_cap)
    give[...] = jnp.where(c == 0, by_cap, turned)


def pair_kernel(place, keep, came, held, rows, captions, out):
    first = place[3] == 0
    m0, m1, s0, s1 = keep[0:1, :], came[0:1, :], keep[2:3, :], came[2:3, :]
    top = jnp.maximum(m0, m1)
    merged = s0 * jnp.exp(m0 - top) + s1 * jnp.exp(m1 - top)
    zero = jnp.zeros((1, TILE), F32)
    out[0:1, :] = jnp.where(first, m0, top)
    out[1:2, :] = jnp.where(first, m1, zero)
    out[2:3, :] = jnp.where(first, s0, merged)
    out[3:4, :] = jnp.where(first, s1, zero)
    out[4:5, :] = keep[4:5, :] + came[4:5, :]
    out[5:6, :] = jnp.maximum(keep[5:6, :], came[5:6, :])
    out[6:8, :] = jnp.zeros((2, TILE), F32)


def merged(own, came):
    top = jnp.maximum(own[0:2, :], came[0:2, :])
    sums = own[2:4, :] * jnp.exp(own[0:2, :] - top) + came[2:4, :] * jnp.exp(came[0:2, :] - top)
    return top, sums, own[4:5, :] + came[4:5, :], jnp.maximum(own[5:6, :], came[5:6, :])


def merge_kernel(own, came, held, rows, captions, out):
    top, sums, total, peak = merged(own[...], came[...])
    out[0:2, :] = top
    out[2:4, :] = sums
    out[4:5, :] = total
    out[5:6, :] = peak
    out[6:8, :] = jnp.zeros((2, TILE), F32)


def first_kernel(place, own, came, held, rows, captions, out):
    lines = lax.broadcasted_iota(jnp.int32, (8, TILE), 0)
    empty = jnp.where(lines < 2, far_below, 0.0)
    top, sums, total, peak = merged(own[...], jnp.where(place[3] == 0, came[...], empty))
    out[0:2, :] = top
    out[2:4, :] = sums
    out[4:5, :] = total
    out[5:6, :] = peak
    out[6:8, :] = jnp.zeros((2, TILE), F32)


def last_kernel(place, own, came, held, rows, captions, out):
    first = place[3] == 0
    lines = lax.broadcasted_iota(jnp.int32, (8, TILE), 0)
    top, sums, total, peak = merged(own[...], came[...])
    lse = top + jnp.log(jnp.where(jnp.logical_or(first, lines[0:2, :] == 0), sums, 1.0))
    both = 0.5 * jnp.sum(lse[0:1, :]) + jnp.where(first, 0.5 * jnp.sum(lse[1:2, :]), 0.0)
    out[0:1, :] = lse[0:1, :]
    out[1:2, :] = jnp.where(first, lse[1:2, :], lse[0:1, :])
    out[2:4, :] = jnp.zeros((2, TILE), F32)
    out[4:5, :] = jnp.broadcast_to(both, (1, TILE)) - total
    out[5:6, :] = peak
    out[6:8, :] = jnp.zeros((2, TILE), F32)


def weight_kernel(
    place, scores, regions, mine, came, matches, w_out, give, kept
):
    z, y, x, c = place[0], place[1], place[2], place[3]
    first_core = c == 0
    row_lse = jnp.where(first_core, mine[0:1, :], came[1:2, :])
    turn = (NX - jnp.where(first_core, y, x)) % NX * 256
    row_lse = pltpu.roll(jnp.broadcast_to(row_lse, (8, TILE)), turn, 1)[0:1, :]
    positive = matches[0:1, :]
    ids = lax.broadcasted_iota(jnp.int32, (BLOCK, TILE), 0)
    for slot in range(8):
        chunk = pl.ds(slot * BLOCK, BLOCK)
        owner = slot_z(slot, z, c)
        lanes = pl.ds(pl.multiple_of(owner * BLOCK, BLOCK), BLOCK)
        cap_line = jnp.where(first_core, came[1:2, lanes], mine[0:1, lanes])
        cap_lse = jnp.concatenate([column(cap_line)] * 8, axis=1)
        first = ((owner * NY + y) * NX + x) * BLOCK
        s = scores[chunk, :]
        weight = 0.5 * (jnp.exp(s - row_lse) + jnp.exp(s - cap_lse))
        weight = weight - jnp.where(ids == positive - first, 1.0, 0.0)
        w_out[chunk, :] = weight.astype(BF)
    scale = region_scale(place, mine, came)
    part = jnp.dot(w_out[0:512, :], regions[...], preferred_element_type=F32) * scale
    nothing = jnp.zeros((8, TILE), F32)
    for at in range(3):
        start = at * 136
        give[start : start + 128, :] = part[at * 128 : (at + 1) * 128, :]
        give[start + 128 : start + 136, :] = nothing
    give[408:472, :] = jnp.where(first_core, part[448:512, :], part[384:448, :])
    give[472:480, :] = nothing
    kept[0:64, :] = jnp.where(first_core, part[384:448, :], part[448:512, :])
    kept[64:72, :] = jnp.where(first_core, digits(mine[4:5, :], z), 0.0)


def digits(value, index):
    high = jnp.floor(value * 2.0**-20)
    rest = value - high * 2.0**20
    middle = jnp.floor(rest * 2.0**-10)
    rest = rest - middle * 2.0**10
    low = jnp.floor(rest)
    last = jnp.floor((rest - low) * 2.0**10)
    lane = lax.broadcasted_iota(jnp.int32, (8, TILE), 1)
    line_at = lax.broadcasted_iota(jnp.int32, (8, TILE), 0)
    which = lane // 16
    digit = jnp.where(
        which == 0, high, jnp.where(which == 1, middle, jnp.where(which == 2, low, last))
    )
    here = jnp.logical_and(line_at == 0, jnp.logical_and(lane < 64, lane % 16 == index))
    return jnp.where(here, digit, 0.0)


def region_scale(place, mine, came):
    region_top = jnp.where(place[3] == 0, came[5:6, :], mine[5:6, :])
    return head_room / jnp.maximum(region_top, tiny)


def caption_kernel(place, weights, regions, mine, came, first, third, second, own):
    first_core = place[3] == 0
    part = jnp.dot(
        weights[512:1024, :], regions[...], preferred_element_type=F32
    ) * region_scale(place, mine, came)
    code = digits(jnp.where(first_core, mine[4:5, :], came[4:5, :]), place[0])
    for at, ref in enumerate((first, third, second)):
        ref[0:128, :] = part[at * 128 : (at + 1) * 128, :]
        ref[128:136, :] = code
    own[0:128, :] = part[384:512, :]
    own[128:136, :] = jnp.where(first_core, code, 0.0)


def region_kernel(place, weights, captions, mine, came, o0, o1, o2, o3):
    first_core = place[3] == 0
    caption_top = jnp.where(first_core, mine[5:6, :], came[5:6, :])
    scale = head_room / jnp.maximum(caption_top, tiny)
    code = digits(
        jnp.where(first_core, came[4:5, :], mine[4:5, :]), place[1] * NX + place[2]
    )
    part = lax.dot_general(
        weights[...], captions[...], (((0,), (0,)), ((), ())), preferred_element_type=F32
    )
    for by, ref in enumerate((o0, o1, o2, o3)):
        ref[0:256, :] = part[by * 256 : (by + 1) * 256, :] * scale
        ref[256:264, :] = code


def pass_kernel(lse, out):
    out[...] = lse[...]


def shards(regions, captions, positive):
    z = lax.axis_index("z")
    y = lax.axis_index("y")
    x = lax.axis_index("col")
    c = lax.axis_index("depth")
    place = jnp.stack([z, y, x, c]).astype(jnp.int32)
    first_core = c == 0
    big = (TILE, FEATURES)

    (part,) = call(
        part_kernel, [((144, FEATURES), BF)], place, regions, positive.reshape(NX, BLOCK)
    )
    (whole,) = call(whole_kernel, [((528, FEATURES), BF)], place, regions, part, us=40.0)
    (text,) = call(text_kernel, [((BLOCK, FEATURES), BF)], captions)

    full = moved(whole, lambda z, y, x, c: (z, y - 1 if c == 0 else y + 1, x, c))
    pair = from_y(part, 2)
    other = moved(pair[0:128], lambda z, y, x, c: (z, y, x ^ 1, c))
    one = along_z(text, -1)
    two = along_z(text, -2)
    (passed,) = call(skip_kernel, [((192, FEATURES), BF)], place, one, two, us=40.0)
    skip = along_z(passed, -2)
    full, other, skip = lax.optimization_barrier((full, other, skip))
    far = swapped(jnp.concatenate([full[256:528], one, two, skip], axis=0))

    small = ((8, TILE), F32)
    scores, region_rows, caption_rows, matches, keep, give = call(
        score_kernel,
        [(big, F32), (big, BF), (big, BF), ((8, TILE), jnp.int32), small, small],
        place, whole, full, far, pair, other, text, one, two, skip,
        us=8.0,
        limit=8 << 20,
    )

    tile = (scores, region_rows, caption_rows)
    (stats,) = call(pair_kernel, [small], place, keep, swapped(give), *tile)

    def partner(bit):
        def target(z, y, x, c):
            if c == 1:
                return (z ^ max(bit, 1) if bit < 3 else NZ - 1 - z, y, x, c)
            if bit % 2 == 0:
                return (z, y ^ 1 if bit == 0 else NY - 1 - y, x, c)
            return (z, y, x ^ 1 if bit == 1 else NX - 1 - x, c)

        return target

    (stats,) = call(first_kernel, [small], place, stats, moved(stats, partner(0)), *tile)
    for bit in (1, 2):
        (stats,) = call(merge_kernel, [small], stats, moved(stats, partner(bit)), *tile)
    (lse,) = call(last_kernel, [small], place, stats, moved(stats, partner(3)), stats, stats, stats)
    came = swapped(lse)
    (lse,) = call(pass_kernel, [small], lse, us=60.0)

    weights, give, kept_half = call(
        weight_kernel,
        [(big, BF), ((480, FEATURES), F32), ((72, FEATURES), F32)],
        place, scores, region_rows, lse, came, matches,
        us=40.0,
        limit=6 << 20,
    )
    got = swapped(give.astype(WIRE))
    r0, r1, r2, r3 = call(
        region_kernel, [((264, FEATURES), F32)] * 4, place, weights, caption_rows, lse, came, us=30.0,
        limit=8 << 20,
    )
    weights, r1, r2, r3 = lax.optimization_barrier(
        (weights, r1.astype(WIRE), r2.astype(WIRE), r3.astype(WIRE))
    )
    block = ((136, FEATURES), F32)
    first, third, second, own = call(
        caption_kernel,
        [block] * 4,
        place, weights, region_rows, lse, came,
        us=20.0,
        limit=6 << 20,
    )
    third = along_z((third + got[136:272].astype(F32)).astype(WIRE), 1)
    skipped = along_z((kept_half + got[408:480].astype(F32)).astype(WIRE), 2)
    ahead = along_z((first + got[0:136].astype(F32)).astype(WIRE), 1)

    def major_from(value, by):
        return moved(
            value, lambda z, y, x, c: (z, y + by, x, c) if c == 0 else (z, y, x + by, c)
        )

    def minor_from(value, by):
        return moved(
            value, lambda z, y, x, c: (z, y, x + by, c) if c == 0 else (z, y + by, x, c)
        )

    nothing = jnp.zeros((GROUP, FEATURES), F32)
    late = skipped.astype(F32)
    late = jnp.where(
        first_core,
        jnp.concatenate([late[0:64], nothing, late[64:72]], axis=0),
        jnp.concatenate([nothing, late], axis=0),
    )
    onward = (second + got[272:408].astype(F32)) + (third.astype(F32) + late)
    passed = along_z(onward.astype(WIRE), 2)
    q2 = major_from(r2, 2)
    q1 = major_from(r1, 1)
    q3 = major_from(r3, 3)
    summed = (r0 + q2.astype(F32)) + (q1.astype(F32) + q3.astype(F32))
    blocks = summed[0:256].reshape(4, GROUP, FEATURES)
    minor = jnp.where(first_core, x, y)

    def piece(by):
        block = lax.dynamic_index_in_dim(blocks, (minor + by) % 4, 0, keepdims=False)
        return jnp.concatenate([block, summed[256:264]], axis=0)

    t2, t1, t3 = (minor_from(piece(by).astype(WIRE), by) for by in (2, 1, 3))
    mine = (own + ahead.astype(F32)) + passed.astype(F32)
    both = mine + swapped(mine)
    all_regions = (piece(0) + t2.astype(F32)) + (t1.astype(F32) + t3.astype(F32))

    caption_top = jnp.where(first_core, lse[5:6, :], came[5:6, :])
    region_top = jnp.where(first_core, came[5:6, :], lse[5:6, :])
    unscale = 1.0 / (head_room * logit_scaling)
    region_grad = all_regions[0:64] * (jnp.maximum(caption_top, tiny) * unscale)
    text_derivative = both[0:128] * (jnp.maximum(region_top, tiny) * unscale)
    numbers = both[128:136, 0:128] + all_regions[64:72, 0:128]
    worth = jnp.exp2(20.0 - 10.0 * (jnp.arange(128) // 16).astype(F32))
    worth = jnp.where(jnp.arange(128) < 64, worth, 0.0)
    mean_objective = jnp.sum(numbers * worth[None, :]) / (NZ * NY * regions.shape[0])
    return mean_objective, region_grad, text_derivative


def solution(mesh):
    grid = Mesh(mesh.devices.reshape(NZ, NY, NX, 2), AXES)
    return jax.shard_map(
        shards,
        mesh=grid,
        in_specs=(P(("z", "y"), None), P(("z", "y", "col"), None), P(("z", "y"))),
        out_specs=(
            P(),
            P(("z", "y", "col", "depth"), None),
            P(("z", "y", "col"), None),
        ),
        check_vma=False,
    )
```

```python
import functools

import jax
import jax.numpy as jnp
from jax import lax
from jax.experimental import pallas as pl
from jax.experimental.pallas import tpu as pltpu
from jax.sharding import Mesh
from jax.sharding import PartitionSpec as P

logit_scaling = 0.07
far_below = -1e30
head_room = 3.5
tiny = 1e-30
AXES = ("z", "y", "col", "depth")
NZ, NY, NX = 8, 4, 4
FEATURES = 1024
GROUP = 64
BLOCK = 128
TILE = 1024
BF = jnp.bfloat16
F32 = jnp.float32
WIRE = jnp.float16
VMEM = pltpu.VMEM
SMEM = pltpu.SMEM


def index_of(z, y, x, c):
    return ((z % NZ * NY + y % NY) * NX + x % NX) * 2 + c


def moved(value, target):
    pairs = []
    for z in range(NZ):
        for y in range(NY):
            for x in range(NX):
                for c in range(2):
                    to = target(z, y, x, c)
                    if to is not None:
                        pairs.append((index_of(z, y, x, c), index_of(*to)))
    return lax.ppermute(value, AXES, pairs)


def swapped(value):
    return moved(value, lambda z, y, x, c: (z, y, x, 1 - c))


def from_y(value, by):
    return moved(value, lambda z, y, x, c: (z, y - by, x, c))


def from_x(value, by):
    return moved(value, lambda z, y, x, c: (z, y, x - by, c))


def along_z(value, by):
    return moved(value, lambda z, y, x, c: (z + by if c == 0 else z - by, y, x, c))


def call(kernel, outs, *args, limit=1 << 20, us=1.0):
    specs = [pl.BlockSpec(memory_space=SMEM if arg.ndim == 1 else VMEM) for arg in args]
    return pl.pallas_call(
        kernel,
        in_specs=specs,
        out_specs=[pl.BlockSpec(memory_space=VMEM) for _ in outs],
        out_shape=[jax.ShapeDtypeStruct(shape, dtype) for shape, dtype in outs],
        cost_estimate=pl.CostEstimate(
            flops=int(us * 1.1e9), bytes_accessed=int(us * 3e6), transcendentals=0
        ),
        compiler_params=pltpu.CompilerParams(vmem_limit_bytes=limit),
    )(*args)


def place_rows(ref, offset, rows):
    ref[pl.ds(pl.multiple_of(offset, GROUP), GROUP), :] = rows


def column(row):
    return jnp.transpose(jnp.broadcast_to(row, (BLOCK, BLOCK)))


def line(col):
    return jnp.transpose(jnp.broadcast_to(col, (BLOCK, BLOCK)))[0:1, :]


WAYS = (-1, -3, -2, 4, 1, 3, 2, 0)


def slot_z(slot, z, c):
    return (z + (1 - 2 * c) * WAYS[slot] + NZ) % NZ


def positives(place, own, full, far, pair):
    y, x, c = place[1], place[2], place[3]
    positive = jnp.zeros((8, TILE), F32)
    for ref, by, start in (
        (own, 0, 512),
        (full, 1 + 2 * c, 512),
        (far, 3 - 2 * c, 258),
        (pair, 2, 128),
    ):
        base = start // 16 * 16
        coded = ref[base : base + 16, :].astype(F32)
        at = start - base
        number = jnp.broadcast_to(
            coded[at : at + 1, :] * 128.0 + coded[at + 1 : at + 2, :], (8, TILE)
        )
        shift = jnp.where(c == 0, by * 256, (y + by) % NY * 64 + TILE - x * 256)
        positive = positive + pltpu.roll(number, shift % TILE, 1)
    return positive[0:1, :].astype(jnp.int32)


def largest(ref):
    best = jnp.abs(ref[0:16, :])
    for start in range(16, TILE, 16):
        best = jnp.maximum(best, jnp.abs(ref[start : start + 16, :]))
    return jnp.max(best.astype(F32))


def coded_matches(place, matches):
    c = place[3]
    lane = lax.broadcasted_iota(jnp.int32, (8, TILE), 1)
    at = lax.broadcasted_iota(jnp.int32, (8, TILE), 0)
    coded = jnp.zeros((8, TILE), F32)
    for step in range(2):
        which = c if step == 0 else 1 - c
        wide = jnp.zeros((8, TILE), F32)
        for xx in range(NX):
            line_of = jnp.concatenate(
                [
                    jnp.broadcast_to(matches[xx : xx + 1, :].astype(F32), (8, BLOCK)),
                    jnp.zeros((8, TILE - BLOCK), F32),
                ],
                axis=1,
            )
            mine = jnp.logical_and(lane >= which * GROUP, lane < which * GROUP + GROUP)
            shift = TILE - which * GROUP + xx * jnp.where(which == 0, 64, 256)
            wide = wide + pltpu.roll(jnp.where(mine, line_of, 0.0), shift % TILE, 1)
        high = jnp.floor(wide * (1.0 / 128.0))
        low = wide - high * 128.0
        coded = jnp.where(at == 2 * step, high, jnp.where(at == 2 * step + 1, low, coded))
    return jnp.concatenate([coded, jnp.zeros((8, TILE), F32)], axis=0).astype(BF)


def part_kernel(place, regions, matches, part):
    x, c = place[2], place[3]
    for at in range(2):
        start = pl.multiple_of(((x % 2 * 2 + at) * 2 + c) * GROUP, GROUP)
        part[at * GROUP : (at + 1) * GROUP, :] = regions[pl.ds(start, GROUP), :].astype(BF)
    part[128:144, :] = coded_matches(place, matches)


def whole_kernel(place, regions, part, whole):
    c = place[3]
    whole[512:528, :] = part[128:144, :]
    for step in range(2):
        which = c if step == 0 else 1 - c
        for xx in range(NX):
            start = pl.multiple_of((xx * 2 + which) * GROUP, GROUP)
            to = (step * NX + xx) * GROUP
            whole[to : to + GROUP, :] = regions[pl.ds(start, GROUP), :].astype(BF)


def text_kernel(captions, text):
    text[...] = captions[...].astype(BF)


def skip_kernel(place, one, two, out):
    out[0:128, :] = one[...]
    out[128:192, :] = two[pl.ds(pl.multiple_of(place[3] * GROUP, GROUP), GROUP), :]


def score_kernel(
    place, own, full, far, pair, other, text, one, two, skip, s_out, r_out, c_out, p_out, keep, give
):
    z, y, x, c = place[0], place[1], place[2], place[3]

    def put(by, xx, rows):
        offset = jnp.where(
            c == 0, by * 256 + xx * 64, (xx + NX - x) % NX * 256 + (y + by) % NY * 64
        )
        place_rows(r_out, offset, rows)

    for ref, by in ((own, 0), (full, 1 + 2 * c), (far, 3 - 2 * c)):
        for xx in range(NX):
            put(by, xx, ref[xx * GROUP : (xx + 1) * GROUP, :])
    for at in range(2):
        rows = pl.ds(at * GROUP, GROUP)
        put(2, x % 2 * 2 + at, pair[rows, :])
        put(2, (1 - x % 2) * 2 + at, other[rows, :])
    c_out[0:128, :] = far[272:400, :]
    c_out[128:256, :] = far[528:656, :]
    c_out[256:384, :] = far[400:528, :]
    place_rows(c_out, 384 + c * GROUP, skip[128:192, :])
    place_rows(c_out, 384 + (1 - c) * GROUP, far[656:720, :])
    c_out[512:640, :] = one[...]
    c_out[640:768, :] = skip[0:128, :]
    c_out[768:896, :] = two[...]
    c_out[896:1024, :] = text[...]

    positive = positives(place, own, full, far, pair)
    p_out[...] = jnp.broadcast_to(positive, (8, TILE))
    regions = r_out[...]
    for part in range(2):
        chunk = pl.ds(part * 512, 512)
        s_out[chunk, :] = lax.dot_general(
            c_out[chunk, :], regions, (((1,), (1,)), ((), ())), preferred_element_type=F32
        ) * (1.0 / logit_scaling)

    row_max = jnp.full((1, TILE), far_below, F32)
    row_sum = jnp.zeros((1, TILE), F32)
    matched = jnp.zeros((1, TILE), F32)
    ids = lax.broadcasted_iota(jnp.int32, (BLOCK, TILE), 0)
    for slot in range(8):
        scores = s_out[slot * BLOCK : (slot + 1) * BLOCK, :]
        owner = slot_z(slot, z, c)
        first = ((owner * NY + y) * NX + x) * BLOCK
        matched = matched + jnp.sum(
            jnp.where(ids == positive - first, scores, 0.0), axis=0, keepdims=True
        )
        new_max = jnp.maximum(row_max, jnp.max(scores, axis=0, keepdims=True))
        row_sum = row_sum * jnp.exp(row_max - new_max) + jnp.sum(
            jnp.exp(scores - new_max), axis=0, keepdims=True
        )
        row_max = new_max
        cap_max = jnp.max(scores, axis=1, keepdims=True)
        cap_sum = jnp.sum(jnp.exp(scores - cap_max), axis=1, keepdims=True)
        lanes = pl.ds(pl.multiple_of(owner * BLOCK, BLOCK), BLOCK)
        give[0:1, lanes] = line(cap_max)
        give[2:3, lanes] = line(cap_sum)

    cap_row_max = give[0:1, :]
    cap_row_sum = give[2:3, :]
    total = jnp.broadcast_to(jnp.sum(matched), (1, TILE))
    caption_top = jnp.broadcast_to(largest(c_out), (1, TILE))
    region_top = jnp.broadcast_to(largest(r_out), (1, TILE))
    zero = jnp.zeros((1, TILE), F32)
    two_zeros = jnp.zeros((2, TILE), F32)
    turned = jnp.concatenate([row_max, zero, row_sum, zero, total, caption_top, two_zeros], axis=0)
    turned = pltpu.roll(turned, jnp.where(c == 0, y, x) * 256, 1)
    by_cap = jnp.concatenate(
        [cap_row_max, zero, cap_row_sum, zero, zero, region_top, two_zeros], axis=0
    )
    keep[...] = jnp.where(c == 0, turned, by_cap)
    give[...] = jnp.where(c == 0, by_cap, turned)


def pair_kernel(place, keep, came, held, rows, captions, out):
    first = place[3] == 0
    m0, m1, s0, s1 = keep[0:1, :], came[0:1, :], keep[2:3, :], came[2:3, :]
    top = jnp.maximum(m0, m1)
    merged = s0 * jnp.exp(m0 - top) + s1 * jnp.exp(m1 - top)
    zero = jnp.zeros((1, TILE), F32)
    out[0:1, :] = jnp.where(first, m0, top)
    out[1:2, :] = jnp.where(first, m1, zero)
    out[2:3, :] = jnp.where(first, s0, merged)
    out[3:4, :] = jnp.where(first, s1, zero)
    out[4:5, :] = keep[4:5, :] + came[4:5, :]
    out[5:6, :] = jnp.maximum(keep[5:6, :], came[5:6, :])
    out[6:8, :] = jnp.zeros((2, TILE), F32)


def merged(own, came):
    top = jnp.maximum(own[0:2, :], came[0:2, :])
    sums = own[2:4, :] * jnp.exp(own[0:2, :] - top) + came[2:4, :] * jnp.exp(came[0:2, :] - top)
    return top, sums, own[4:5, :] + came[4:5, :], jnp.maximum(own[5:6, :], came[5:6, :])


def merge_kernel(own, came, held, rows, captions, out):
    top, sums, total, peak = merged(own[...], came[...])
    out[0:2, :] = top
    out[2:4, :] = sums
    out[4:5, :] = total
    out[5:6, :] = peak
    out[6:8, :] = jnp.zeros((2, TILE), F32)


def first_kernel(place, own, came, held, rows, captions, out):
    lines = lax.broadcasted_iota(jnp.int32, (8, TILE), 0)
    empty = jnp.where(lines < 2, far_below, 0.0)
    top, sums, total, peak = merged(own[...], jnp.where(place[3] == 0, came[...], empty))
    out[0:2, :] = top
    out[2:4, :] = sums
    out[4:5, :] = total
    out[5:6, :] = peak
    out[6:8, :] = jnp.zeros((2, TILE), F32)


def last_kernel(place, own, came, held, rows, captions, out):
    first = place[3] == 0
    lines = lax.broadcasted_iota(jnp.int32, (8, TILE), 0)
    top, sums, total, peak = merged(own[...], came[...])
    lse = top + jnp.log(jnp.where(jnp.logical_or(first, lines[0:2, :] == 0), sums, 1.0))
    both = 0.5 * jnp.sum(lse[0:1, :]) + jnp.where(first, 0.5 * jnp.sum(lse[1:2, :]), 0.0)
    out[0:1, :] = lse[0:1, :]
    out[1:2, :] = jnp.where(first, lse[1:2, :], lse[0:1, :])
    out[2:4, :] = jnp.zeros((2, TILE), F32)
    out[4:5, :] = jnp.broadcast_to(both, (1, TILE)) - total
    out[5:6, :] = peak
    out[6:8, :] = jnp.zeros((2, TILE), F32)


def weight_kernel(
    place, scores, regions, mine, came, matches, w_out, give, kept
):
    z, y, x, c = place[0], place[1], place[2], place[3]
    first_core = c == 0
    row_lse = jnp.where(first_core, mine[0:1, :], came[1:2, :])
    turn = (NX - jnp.where(first_core, y, x)) % NX * 256
    row_lse = pltpu.roll(jnp.broadcast_to(row_lse, (8, TILE)), turn, 1)[0:1, :]
    positive = matches[0:1, :]
    ids = lax.broadcasted_iota(jnp.int32, (BLOCK, TILE), 0)
    for slot in range(8):
        chunk = pl.ds(slot * BLOCK, BLOCK)
        owner = slot_z(slot, z, c)
        lanes = pl.ds(pl.multiple_of(owner * BLOCK, BLOCK), BLOCK)
        cap_line = jnp.where(first_core, came[1:2, lanes], mine[0:1, lanes])
        cap_lse = jnp.concatenate([column(cap_line)] * 8, axis=1)
        first = ((owner * NY + y) * NX + x) * BLOCK
        s = scores[chunk, :]
        weight = 0.5 * (jnp.exp(s - row_lse) + jnp.exp(s - cap_lse))
        weight = weight - jnp.where(ids == positive - first, 1.0, 0.0)
        w_out[chunk, :] = weight.astype(BF)
    scale = region_scale(place, mine, came)
    part = jnp.dot(w_out[0:512, :], regions[...], preferred_element_type=F32) * scale
    nothing = jnp.zeros((8, TILE), F32)
    for at in range(3):
        start = at * 136
        give[start : start + 128, :] = part[at * 128 : (at + 1) * 128, :]
        give[start + 128 : start + 136, :] = nothing
    give[408:472, :] = jnp.where(first_core, part[448:512, :], part[384:448, :])
    give[472:480, :] = nothing
    kept[0:64, :] = jnp.where(first_core, part[384:448, :], part[448:512, :])
    kept[64:72, :] = jnp.where(first_core, digits(mine[4:5, :], z), 0.0)


def digits(value, index):
    high = jnp.floor(value * 2.0**-20)
    rest = value - high * 2.0**20
    middle = jnp.floor(rest * 2.0**-10)
    rest = rest - middle * 2.0**10
    low = jnp.floor(rest)
    last = jnp.floor((rest - low) * 2.0**10)
    lane = lax.broadcasted_iota(jnp.int32, (8, TILE), 1)
    line_at = lax.broadcasted_iota(jnp.int32, (8, TILE), 0)
    which = lane // 16
    digit = jnp.where(
        which == 0, high, jnp.where(which == 1, middle, jnp.where(which == 2, low, last))
    )
    here = jnp.logical_and(line_at == 0, jnp.logical_and(lane < 64, lane % 16 == index))
    return jnp.where(here, digit, 0.0)


def region_scale(place, mine, came):
    region_top = jnp.where(place[3] == 0, came[5:6, :], mine[5:6, :])
    return head_room / jnp.maximum(region_top, tiny)


def caption_kernel(place, weights, regions, mine, came, first, third, second, own):
    first_core = place[3] == 0
    part = jnp.dot(
        weights[512:1024, :], regions[...], preferred_element_type=F32
    ) * region_scale(place, mine, came)
    code = digits(jnp.where(first_core, mine[4:5, :], came[4:5, :]), place[0])
    for at, ref in enumerate((first, third, second)):
        ref[0:128, :] = part[at * 128 : (at + 1) * 128, :]
        ref[128:136, :] = code
    own[0:128, :] = part[384:512, :]
    own[128:136, :] = jnp.where(first_core, code, 0.0)


def region_kernel(place, weights, captions, mine, came, o0, o1, o2, o3):
    first_core = place[3] == 0
    caption_top = jnp.where(first_core, mine[5:6, :], came[5:6, :])
    scale = head_room / jnp.maximum(caption_top, tiny)
    code = digits(
        jnp.where(first_core, came[4:5, :], mine[4:5, :]), place[1] * NX + place[2]
    )
    part = lax.dot_general(
        weights[...], captions[...], (((0,), (0,)), ((), ())), preferred_element_type=F32
    )
    for by, ref in enumerate((o0, o1, o2, o3)):
        ref[0:256, :] = part[by * 256 : (by + 1) * 256, :] * scale
        ref[256:264, :] = code


def pass_kernel(lse, out):
    out[...] = lse[...]


def shards(regions, captions, positive):
    z = lax.axis_index("z")
    y = lax.axis_index("y")
    x = lax.axis_index("col")
    c = lax.axis_index("depth")
    place = jnp.stack([z, y, x, c]).astype(jnp.int32)
    first_core = c == 0
    big = (TILE, FEATURES)

    (part,) = call(
        part_kernel, [((144, FEATURES), BF)], place, regions, positive.reshape(NX, BLOCK)
    )
    (whole,) = call(whole_kernel, [((528, FEATURES), BF)], place, regions, part, us=40.0)
    (text,) = call(text_kernel, [((BLOCK, FEATURES), BF)], captions)

    full = moved(whole, lambda z, y, x, c: (z, y - 1 if c == 0 else y + 1, x, c))
    pair = from_y(part, 2)
    other = moved(pair[0:128], lambda z, y, x, c: (z, y, x ^ 1, c))
    one = along_z(text, -1)
    two = along_z(text, -2)
    (passed,) = call(skip_kernel, [((192, FEATURES), BF)], place, one, two, us=40.0)
    skip = along_z(passed, -2)
    full, other, skip = lax.optimization_barrier((full, other, skip))
    far = swapped(jnp.concatenate([full[256:528], one, two, skip], axis=0))

    small = ((8, TILE), F32)
    scores, region_rows, caption_rows, matches, keep, give = call(
        score_kernel,
        [(big, F32), (big, BF), (big, BF), ((8, TILE), jnp.int32), small, small],
        place, whole, full, far, pair, other, text, one, two, skip,
        us=8.0,
        limit=8 << 20,
    )

    tile = (scores, region_rows, caption_rows)
    (stats,) = call(pair_kernel, [small], place, keep, swapped(give), *tile)

    def partner(bit):
        def target(z, y, x, c):
            if c == 1:
                return (z ^ max(bit, 1) if bit < 3 else NZ - 1 - z, y, x, c)
            if bit % 2 == 0:
                return (z, y ^ 1 if bit == 0 else NY - 1 - y, x, c)
            return (z, y, x ^ 1 if bit == 1 else NX - 1 - x, c)

        return target

    (stats,) = call(first_kernel, [small], place, stats, moved(stats, partner(0)), *tile)
    for bit in (1, 2):
        (stats,) = call(merge_kernel, [small], stats, moved(stats, partner(bit)), *tile)
    (lse,) = call(last_kernel, [small], place, stats, moved(stats, partner(3)), stats, stats, stats)
    came = swapped(lse)
    (lse,) = call(pass_kernel, [small], lse, us=60.0)

    weights, give, kept_half = call(
        weight_kernel,
        [(big, BF), ((480, FEATURES), F32), ((72, FEATURES), F32)],
        place, scores, region_rows, lse, came, matches,
        us=40.0,
        limit=6 << 20,
    )
    got = swapped(give.astype(WIRE))
    r0, r1, r2, r3 = call(
        region_kernel, [((264, FEATURES), F32)] * 4, place, weights, caption_rows, lse, came, us=30.0,
        limit=8 << 20,
    )
    weights, r1, r2, r3 = lax.optimization_barrier(
        (weights, r1.astype(WIRE), r2.astype(WIRE), r3.astype(WIRE))
    )
    block = ((136, FEATURES), F32)
    first, third, second, own = call(
        caption_kernel,
        [block] * 4,
        place, weights, region_rows, lse, came,
        us=20.0,
        limit=6 << 20,
    )
    third = along_z((third + got[136:272].astype(F32)).astype(WIRE), 1)
    skipped = along_z((kept_half + got[408:480].astype(F32)).astype(WIRE), 2)
    first = (first + got[0:136].astype(F32)).astype(WIRE)

    def major_from(value, by):
        return moved(
            value, lambda z, y, x, c: (z, y + by, x, c) if c == 0 else (z, y, x + by, c)
        )

    def minor_from(value, by):
        return moved(
            value, lambda z, y, x, c: (z, y, x + by, c) if c == 0 else (z, y + by, x, c)
        )

    nothing = jnp.zeros((GROUP, FEATURES), F32)
    late = skipped.astype(F32)
    late = jnp.where(
        first_core,
        jnp.concatenate([late[0:64], nothing, late[64:72]], axis=0),
        jnp.concatenate([nothing, late], axis=0),
    )
    onward = (second + got[272:408].astype(F32)) + (third.astype(F32) + late)
    onward, first = lax.optimization_barrier((onward.astype(WIRE), first))
    passed = along_z(onward, 2)
    ahead = along_z(first, 1)
    q2 = major_from(r2, 2)
    q1 = major_from(r1, 1)
    q3 = major_from(r3, 3)
    summed = (r0 + q2.astype(F32)) + (q1.astype(F32) + q3.astype(F32))
    blocks = summed[0:256].reshape(4, GROUP, FEATURES)
    minor = jnp.where(first_core, x, y)

    def piece(by):
        block = lax.dynamic_index_in_dim(blocks, (minor + by) % 4, 0, keepdims=False)
        return jnp.concatenate([block, summed[256:264]], axis=0)

    t2, t1, t3 = (minor_from(piece(by).astype(WIRE), by) for by in (2, 1, 3))
    mine = (own + ahead.astype(F32)) + passed.astype(F32)
    both = mine + swapped(mine)
    all_regions = (piece(0) + t2.astype(F32)) + (t1.astype(F32) + t3.astype(F32))

    caption_top = jnp.where(first_core, lse[5:6, :], came[5:6, :])
    region_top = jnp.where(first_core, came[5:6, :], lse[5:6, :])
    unscale = 1.0 / (head_room * logit_scaling)
    region_grad = all_regions[0:64] * (jnp.maximum(caption_top, tiny) * unscale)
    text_derivative = both[0:128] * (jnp.maximum(region_top, tiny) * unscale)
    numbers = both[128:136, 0:128] + all_regions[64:72, 0:128]
    worth = jnp.exp2(20.0 - 10.0 * (jnp.arange(128) // 16).astype(F32))
    worth = jnp.where(jnp.arange(128) < 64, worth, 0.0)
    mean_objective = jnp.sum(numbers * worth[None, :]) / (NZ * NY * regions.shape[0])
    return mean_objective, region_grad, text_derivative


def solution(mesh):
    grid = Mesh(mesh.devices.reshape(NZ, NY, NX, 2), AXES)
    return jax.shard_map(
        shards,
        mesh=grid,
        in_specs=(P(("z", "y"), None), P(("z", "y", "col"), None), P(("z", "y"))),
        out_specs=(
            P(),
            P(("z", "y", "col", "depth"), None),
            P(("z", "y", "col"), None),
        ),
        check_vma=False,
    )
```
